128 devices in a mesh: vocab: 16 (over y, z), feat: 8 (over x, core).
Axes of the slice: x: 4, y: 4, z: 4, core: 2. Of those that a mesh axis runs over, the one named last changes fastest.
Arguments:
- hidden: bfloat16 [2048, 4096], P('feat'), may hold values from -64 to 64
- out_head: bfloat16 [131072, 4096], P(('vocab', 'feat')), may hold values from -0.28125 to 0.28125
- out_proj: bfloat16 [131072, 128], P(('vocab', 'feat')), may hold values from -5 to 5
- in_proj: bfloat16 [4096, 128], replicated, may hold values from -0.09375 to 0.09375
- targets: int32 [2048], replicated, may hold values from 0 to 131071
- seq_ids: int32 [2048], replicated, may hold values from 0 to 15, never falling along the last dimension, each value on 1 to 256 neighbouring positions
- grad_store: bfloat16 [32768, 16384], P('vocab', 'feat'), may hold values from -0.01953125 to 0.01953125
Outputs:
- influence: float32 [32768, 16], P(('vocab', 'feat'))
The draws below stay inside these ranges and needn't reach their ends.
All inputs are finite; a program needn't handle non-finite values.
Results may differ from the reference program's by a relative error of at most 0.003.
Values may be sent and summed in bfloat16 or wider, within the bound.
No kernel may reach another device: no remote copies, remote signals or barrier semaphores. Data moves between devices by JAX's collectives and lax.ppermute only.
A program may use at most 128 MiB of HBM per device.

```python
import math
import jax
import jax.numpy as jnp
import numpy as np
from jax import lax

D = 4096
R = 128
SEQS = 16
VOCAB = 131072
TOKENS = 2048
EXAMPLES = 32768
FEATS = 16384


def head_rows(key, row_ids):
    base_key = jax.random.fold_in(key, 7)

    def single(row_id):
        values = jax.random.normal(jax.random.fold_in(base_key, row_id), (D,), jnp.float32)
        return jnp.clip(values, -6.0, 6.0) * (3.0 / math.sqrt(D))
    return jax.vmap(single)(row_ids)


def draw_out_head(key, part):
    return head_rows(key, jnp.arange(VOCAB, dtype=jnp.int32)).astype(jnp.bfloat16)


def draw_hidden(key, part):
    values = jnp.clip(jax.random.normal(jax.random.fold_in(key, 3), (TOKENS, D), jnp.float32), -5.0, 5.0)
    return values.astype(jnp.bfloat16)


def place_ends(drawn, rng, low, high):
    longest = drawn.shape.index(max(drawn.shape))
    spots = []
    for shift in (0, 1):
        where = [jax.random.randint(jax.random.fold_in(rng, axis), (), 0, length) for axis, length in enumerate(drawn.shape)]
        where[longest] = (where[longest] + shift) % drawn.shape[longest]
        spots.append(tuple(where))
    return drawn.at[spots[0]].set(low).at[spots[1]].set(high)


def with_spikes(result, stream_key, source, target, blocks, factor):
    owner, partner = [(jnp.arange(result.shape[position]) // (result.shape[position] // blocks)).reshape([-1 if axis == position else 1 for axis in range(result.ndim)]) for position in (source, target)]
    chosen = jax.random.permutation(stream_key, blocks)[partner]
    strong = (owner == chosen) | (owner == (partner + blocks // 2) % blocks)
    return jnp.where(strong, factor * result, result)


def block_scale(own_key, shape, split, smallest, top_value):
    def one(position, parts):
        draws = jax.random.uniform(jax.random.fold_in(jax.random.fold_in(own_key, 6), position), (parts,), jnp.float32, smallest / len(split), top_value / len(split))
        return jnp.repeat(jnp.exp(draws), shape[position] // parts).reshape((-1,) + (1,) * (len(shape) - position - 1))

    level = one(*split[0])
    for cut in split[1:]:
        level = level * one(*cut)
    return level


def split_up(amount, total, most, lean):
    loads = [(1 << 20) // math.isqrt(standing ** lean) + 1 for standing in range(2, amount + 1)]
    spare, holding = total - most - (amount - 1), [1] * (amount - 1)
    while spare > 0:
        candidates = [i for i in range(amount - 1) if holding[i] < most]
        pool, remaining = sum([loads[i] for i in candidates]), spare
        for i in candidates:
            more = min(most - holding[i], max(1, remaining * loads[i] // pool), spare)
            holding[i] = holding[i] + more
            spare = spare - more
    return np.array([most] + holding)


def ragged_sizes(key, number_of, total, reach, lean):
    if number_of == 2:
        one = jax.random.randint(key, (), max(1, total - reach), min(reach, total - 1) + 1)
        return jnp.stack([one, total - one])
    sizes = jnp.asarray(split_up(number_of, total, reach, lean), jnp.int32)
    couples = (number_of - 1) // 2
    donor, sink = sizes[1:1 + 2 * couples:2], sizes[2:2 + 2 * couples:2]
    margin = jnp.minimum(donor - 1, reach - sink)
    moved = jax.random.randint(jax.random.fold_in(key, 1), (couples,), 0, 1 << 20) % (margin + 1)
    sizes = sizes.at[1:1 + 2 * couples:2].set(donor - moved).at[2:2 + 2 * couples:2].set(sink + moved)
    return sizes[jax.random.permutation(jax.random.fold_in(key, 2), number_of)]


def bell_draw(key, shape, scale, limit, cuts=(), kind=jnp.bfloat16):
    drawn = jax.random.normal(key, shape, jnp.float32) * scale
    if len(cuts) > 0:
        drawn = block_scale(key, shape, cuts, -0.22, 0.18) * drawn
    return jnp.clip(drawn, min=-limit, max=limit).astype(kind)


def gaussian_with(key, shape, width, bound, split, heavy, kind=jnp.bfloat16):
    entries = width * jax.random.normal(key, shape, jnp.float32)
    if split:
        entries = entries * block_scale(key, shape, split, -0.22, 0.18)
    return jnp.clip(with_spikes(entries, jax.random.fold_in(key, 3), *heavy), -bound, bound).astype(kind)


def setup_inputs(seed: int = 0) -> dict:
    keys = jax.random.split(jax.random.key(seed), 8)
    return {
        "hidden": draw_hidden(jax.random.fold_in(keys[7], 71), 0),
        "out_head": draw_out_head(jax.random.fold_in(keys[7], 71), 0),
        "out_proj": bell_draw(keys[2], (VOCAB, R), 1.0, 5.0, ((0, 128),)),
        "in_proj": bell_draw(keys[3], (D, R), D ** -0.5, 0.09375),
        "targets": place_ends(jax.random.randint(keys[4], (TOKENS,), 0, VOCAB), jax.random.fold_in(keys[4], 1), 0, VOCAB - 1).astype(jnp.int32),
        "seq_ids": jnp.searchsorted(jnp.cumsum(ragged_sizes(keys[5], SEQS, TOKENS, 2 * TOKENS // SEQS, 0)), jnp.arange(TOKENS), side="right").astype(jnp.int32),
        "grad_store": gaussian_with(keys[6], (EXAMPLES, FEATS), (1.0 / (8.0 * R)), 0.01953125, ((0, 16), (1, 8)), (1, 0, 16, 2.0)),
    }


def reference(hidden, out_head, out_proj, in_proj, targets, seq_ids, grad_store):
    logits = jnp.dot(hidden, out_head.T, preferred_element_type=jnp.float32)
    row_max = jnp.max(logits, axis=1, keepdims=True)
    expval = jnp.exp(logits - row_max)
    row_sum = jnp.sum(expval, axis=1, keepdims=True)
    columns = jnp.arange(VOCAB, dtype=jnp.int32)
    onehot = (targets[:, None] == columns[None, :]).astype(jnp.float32)
    residual = (expval / row_sum - onehot).astype(jnp.bfloat16)
    out_side = jnp.dot(residual, out_proj, preferred_element_type=jnp.float32)
    in_side = jnp.dot(hidden, in_proj, preferred_element_type=jnp.float32)
    member = (seq_ids[:, None] == jnp.arange(SEQS, dtype=jnp.int32)[None, :]).astype(jnp.float32)
    query_grads = jnp.einsum("ts,ti,tj->sij", member, out_side, in_side, precision=lax.Precision.HIGHEST)
    query_grads = query_grads.reshape(SEQS, R * R).astype(jnp.bfloat16)
    return jnp.dot(grad_store, query_grads.T, preferred_element_type=jnp.float32)
```

```python
import functools

import jax
import jax.numpy as jnp
from jax import lax
from jax.experimental import pallas as pl
from jax.experimental.pallas import tpu as pltpu
from jax.sharding import Mesh
from jax.sharding import PartitionSpec as P

SEQS = 16
ALL = ("y", "z", "x", "c")
TILE = 256
BF = jnp.bfloat16
F32 = jnp.float32


def index(y, z, x, c):
    return (((y % 4) * 4 + z % 4) * 4 + x % 4) * 2 + c


def move(value, target):
    pairs = [
        (index(y, z, x, c), index(*target(y, z, x, c)))
        for y in range(4)
        for z in range(4)
        for x in range(4)
        for c in range(2)
    ]
    return lax.ppermute(value, ALL, pairs)


def along_x(y, z, x, c):
    return (y, z, x + 1 - 2 * c, c)


def along_x_crossed(y, z, x, c):
    return (y, z, x - 1 + 2 * c, 1 - c)


def along_y(y, z, x, c):
    return (y + 1 - 2 * c, z, x, c)


def along_z(y, z, x, c):
    return (y, z + 1 - 2 * c, x, c)


def to_sibling(y, z, x, c):
    return (y, z, x, 1 - c)


def flash_kernel(sizes, tiles, *refs):
    count = len(sizes)
    pieces = refs[:count]
    own_ref, sib_ref, proj_ref, in_ref, out_ref, lse_ref, side_ref, tok, scores = refs[count:]
    step = pl.program_id(0)

    @pl.when(step == 0)
    def _():
        at = 0
        for size, piece in zip(sizes, pieces):
            tok[at : at + size, :] = piece[...]
            at += size
        side_ref[...] = jnp.dot(tok[...], in_ref[...], preferred_element_type=F32)

    dims = (((1,), (1,)), ((), ()))

    @pl.when(step < tiles // 2)
    def _():
        scores[step] = lax.dot_general(tok[...], own_ref[...], dims, preferred_element_type=F32)

    @pl.when(step >= tiles // 2)
    def _():
        scores[step] = lax.dot_general(tok[...], sib_ref[...], dims, preferred_element_type=F32)

    @pl.when(step == tiles - 1)
    def _():
        best = scores[0]
        for t in range(1, tiles):
            best = jnp.maximum(best, scores[t])
        best = jnp.max(best, axis=1, keepdims=True)
        total = None
        mixed = None
        for t in range(tiles):
            power = jnp.exp(scores[t] - best)
            total = power if t == 0 else total + power
            part = jnp.dot(
                power.astype(BF), proj_ref[t * TILE : (t + 1) * TILE, :], preferred_element_type=F32
            )
            mixed = part if t == 0 else mixed + part
        total = jnp.sum(total, axis=1, keepdims=True)
        out_ref[...] = mixed / total
        lse_ref[...] = jnp.broadcast_to(best + jnp.log(total), lse_ref.shape)


def flash(pieces, own, sib, proj, in_proj):
    sizes = tuple(p.shape[0] for p in pieces)
    n = sum(sizes)
    depth = own.shape[1]
    rows = own.shape[0]
    rank = proj.shape[1]
    half = rows // TILE
    tiles = 2 * half
    whole = lambda shape: pl.BlockSpec(shape, lambda i: (0, 0))
    return pl.pallas_call(
        functools.partial(flash_kernel, sizes, tiles),
        grid=(tiles,),
        in_specs=[whole(p.shape) for p in pieces]
        + [
            pl.BlockSpec((TILE, depth), lambda i: (jnp.minimum(i, half - 1), 0)),
            pl.BlockSpec((TILE, depth), lambda i: (jnp.maximum(i - half, 0), 0)),
            whole(proj.shape),
            whole(in_proj.shape),
        ],
        out_specs=[whole((n, rank))] * 3,
        out_shape=[jax.ShapeDtypeStruct((n, rank), F32)] * 3,
        scratch_shapes=[pltpu.VMEM((n, depth), BF), pltpu.VMEM((tiles, n, TILE), F32)],
        compiler_params=pltpu.CompilerParams(vmem_limit_bytes=48 * 1024 * 1024),
        cost_estimate=pl.CostEstimate(
            flops=2 * n * 2 * rows * depth, bytes_accessed=2 * rows * depth * 2, transcendentals=0
        ),
    )(*pieces, own, sib, proj, in_proj)


def hot_kernel(where, targets_ref, proj_ref, out_ref):
    local = out_ref.shape[1]
    rows = proj_ref.shape[1]
    half = rows // 2
    total = None
    for t in range(rows // TILE):
        first = t * TILE
        base = where[0] + first if first < half else where[1] + first - half
        ids = base + lax.broadcasted_iota(jnp.int32, (TILE, local), 0)
        hot = jnp.where(ids == targets_ref[...], 1.0, 0.0).astype(BF)
        part = jnp.dot(proj_ref[:, first : first + TILE], hot, preferred_element_type=F32)
        total = part if t == 0 else total + part
    out_ref[...] = total


def hot_rows(where, targets, proj_t):
    return pl.pallas_call(
        hot_kernel,
        in_specs=[
            pl.BlockSpec(memory_space=pltpu.SMEM),
            pl.BlockSpec(memory_space=pltpu.VMEM),
            pl.BlockSpec(memory_space=pltpu.VMEM),
        ],
        out_specs=pl.BlockSpec(memory_space=pltpu.VMEM),
        out_shape=jax.ShapeDtypeStruct((proj_t.shape[0], targets.shape[1]), F32),
        compiler_params=pltpu.CompilerParams(vmem_limit_bytes=32 * 1024 * 1024),
        cost_estimate=pl.CostEstimate(
            flops=2 * 128 * 2048 * 1024, bytes_accessed=1 << 20, transcendentals=0
        ),
    )(where, targets, proj_t)


def pack_kernel(place, *refs):
    outs, lses, sides = refs[0:3], refs[3:6], refs[6:9]
    hot_ref, send_ref, side_ref, out_nat, lse_nat = refs[9:]
    k = place[0]
    spot = [place[1], place[2], place[3], place[4]]

    def put(slot, quarter, source, start, rows, into=0):
        for h in range(rows // 32):
            group = quarter * 2 + into + h
            at = slice(start + 32 * h, start + 32 * h + 32)
            out_nat[group, spot[slot]] = outs[source][at, :]
            lse_nat[group, spot[slot]] = lses[source][at, :]
            side_ref[group, spot[slot]] = sides[source][at, :]

    ky, kz, kd = k ^ 2, k ^ 1, k ^ 3
    for q in range(4):
        put(0, q, 0, 64 * q, 64)
    for n, (slot, quarter) in enumerate(
        [(1, k), (2, k), (1, ky), (2, ky), (1, kz), (2, kz), (3, k), (1, kd)]
    ):
        put(slot, quarter, 1, 64 * n, 64)
    put(3, ky, 2, 0, 64)
    put(2, kd, 2, 64, 32)
    put(3, kz, 2, 96, 64)
    put(2, kd, 2, 160, 32, into=1)
    put(3, kd, 2, 192, 64)

    for group in range(8):
        mixed = jnp.transpose(out_nat[group].reshape(128, 128)).reshape(16, 8, 128)
        lse = jnp.transpose(lse_nat[group].reshape(128, 128))[0:8, :]
        high = lse.astype(BF).astype(F32)
        rest = lse - high
        middle = rest.astype(BF).astype(F32)
        low = rest - middle
        line = lax.broadcasted_iota(jnp.int32, (8, 128), 0)
        stats = jnp.where(
            line == 0, high, jnp.where(line == 1, middle, jnp.where(line == 2, low, 0.0))
        )
        hot = hot_ref[:, group * 128 : group * 128 + 128].reshape(16, 8, 128)
        for part in range(16):
            to = (2 * group + part % 2) * 8 + part // 2
            send_ref[to] = jnp.concatenate([mixed[part], hot[part], stats], axis=0).astype(BF)


def pack(place, results, hot):
    outs, lses, sides = zip(*results)
    return pl.pallas_call(
        pack_kernel,
        in_specs=[pl.BlockSpec(memory_space=pltpu.SMEM)]
        + [pl.BlockSpec(memory_space=pltpu.VMEM)] * 10,
        out_specs=[pl.BlockSpec(memory_space=pltpu.VMEM)] * 2,
        out_shape=[
            jax.ShapeDtypeStruct((128, 24, 128), BF),
            jax.ShapeDtypeStruct((8, 4, 32, 128), F32),
        ],
        scratch_shapes=[pltpu.VMEM((8, 4, 32, 128), F32)] * 2,
        compiler_params=pltpu.CompilerParams(vmem_limit_bytes=32 * 1024 * 1024),
    )(place, *outs, *lses, *sides, hot)


def merge_kernel(got_ref, out_ref):
    lse = (
        got_ref[:, 16:24, :].astype(F32)
    )
    lse = lse[:, 0:1, :] + lse[:, 1:2, :] + lse[:, 2:3, :]
    source = lax.broadcasted_iota(jnp.int32, (128, 1, 128), 0)
    lane = lax.broadcasted_iota(jnp.int32, (128, 1, 128), 2)
    x = lax.div(lax.rem(source, 8), 2)
    c = lax.rem(source, 2)
    other = lax.div(lane, 32) == lax.rem(x + 1, 4)
    kind = jnp.where(other, 1 - c, c)
    halves = []
    for which in range(2):
        mine = kind == which
        best = jnp.max(jnp.where(mine, lse, -3.0e38), axis=0, keepdims=True)
        weight = jnp.where(mine, jnp.exp(jnp.minimum(lse - best, 0.0)), 0.0)
        total = jnp.sum(weight, axis=0)
        mixed = jnp.sum(weight * got_ref[:, 0:8, :].astype(F32), axis=0)
        hot = jnp.sum(jnp.where(mine, got_ref[:, 8:16, :].astype(F32), 0.0), axis=0)
        halves.append(mixed / total - hot)
    both = jnp.concatenate(halves, axis=1)
    for copy in range(16):
        out_ref[copy] = both


def merge(got):
    return pl.pallas_call(
        merge_kernel,
        in_specs=[pl.BlockSpec(memory_space=pltpu.VMEM)],
        out_specs=pl.BlockSpec(memory_space=pltpu.VMEM),
        out_shape=jax.ShapeDtypeStruct((16, 8, 256), F32),
        compiler_params=pltpu.CompilerParams(vmem_limit_bytes=32 * 1024 * 1024),
    )(got)


def score_kernel(flags, out_ref, own_ref, sib_ref, seq_ref, store_ref, result_ref, grads):
    @pl.when(pl.program_id(0) == 0)
    def _():
        total = jnp.zeros((256, 128), F32)
        for group in range(8):
            out = jnp.concatenate([out_ref[2 * group], out_ref[2 * group + 1]], axis=0)
            ids = seq_ref[group : group + 1, :]
            member = lax.broadcasted_iota(jnp.int32, (16, 256), 0) == ids
            spread = jnp.where(member[None, :, :], out[:, None, :], 0.0).reshape(256, 256)
            first, second = [], []
            for spot in range(4):
                own, sib = own_ref[group, spot], sib_ref[group, spot]
                keep = flags[spot] == 0
                first.append(jnp.where(keep, own, sib))
                second.append(jnp.where(keep, sib, own))
            side = jnp.concatenate(first + second, axis=0)
            spread_high = spread.astype(BF)
            spread_low = (spread - spread_high.astype(F32)).astype(BF)
            side_high = side.astype(BF)
            side_low = (side - side_high.astype(F32)).astype(BF)
            for a, b in (
                (spread_high, side_high),
                (spread_high, side_low),
                (spread_low, side_high),
            ):
                total += jnp.dot(a, b, preferred_element_type=F32)
        for i in range(16):
            grads[:, i * 128 : (i + 1) * 128] = total[i * 16 : (i + 1) * 16, :].astype(BF)

    result_ref[0] = lax.dot_general(
        grads[...], store_ref[...], (((1,), (1,)), ((), ())), preferred_element_type=F32
    )


def score(flags, out, own, sib, seq, store):
    fixed = lambda shape: pl.BlockSpec(shape, lambda i: (0,) * len(shape))
    return pl.pallas_call(
        score_kernel,
        grid=(8,),
        in_specs=[
            pl.BlockSpec(memory_space=pltpu.SMEM),
            fixed(out.shape),
            fixed(own.shape),
            fixed(sib.shape),
            fixed(seq.shape),
            pl.BlockSpec((store.shape[0] // 8, store.shape[1]), lambda i: (i, 0)),
        ],
        out_specs=pl.BlockSpec((1, SEQS, 256), lambda i: (i, 0, 0)),
        out_shape=jax.ShapeDtypeStruct((8, SEQS, 256), F32),
        scratch_shapes=[pltpu.VMEM((SEQS, store.shape[1]), BF)],
        compiler_params=pltpu.CompilerParams(vmem_limit_bytes=32 * 1024 * 1024),
    )(flags, out, own, sib, seq, store)


def finish_kernel(got_ref, out_ref):
    total = got_ref[0]
    for source in range(1, 8):
        total = total + got_ref[source]
    out_ref[...] = jnp.transpose(total)


def finish(got):
    return pl.pallas_call(
        finish_kernel,
        in_specs=[pl.BlockSpec(memory_space=pltpu.VMEM)],
        out_specs=pl.BlockSpec(memory_space=pltpu.VMEM),
        out_shape=jax.ShapeDtypeStruct((256, SEQS), F32),
    )(got)


def by_place(per_token):
    table = per_token.reshape(4, 2, 256)
    return jnp.stack([table[:, 0], jnp.roll(table[:, 1], 2, axis=0)])


def on_device(hidden, out_head, out_proj, in_proj, targets, seq_ids, grad_store):
    y, z, x, c = (lax.axis_index(name) for name in ALL)
    k = 2 * (y % 2) + z % 2
    sign = 1 - 2 * c
    rows = out_head.shape[0]

    mine = lax.dynamic_slice_in_dim(hidden, k * 64, 64, 0)
    mine_d = lax.dynamic_slice_in_dim(hidden, (3 - k) * 64, 64, 0)

    near_a = move(mine, along_x)
    near_b = move(mine, along_x_crossed)
    head_sib = move(out_head, to_sibling)
    proj_sib = move(out_proj, to_sibling)
    mine_d, near_a = lax.optimization_barrier((mine_d, near_a))
    far_k = move(near_a, along_x)
    near_a_y = move(near_a, along_y)
    near_a_z = move(near_a, along_z)
    near_a_d = move(mine_d, along_x)
    near_b_y = move(near_b, along_y)
    near_b_z = move(near_b, along_z)
    last_y = move(jnp.concatenate([far_k, near_b_z[:32]], axis=0), along_y)
    last_z = move(jnp.concatenate([far_k, near_b_y[32:]], axis=0), along_z)
    far_d = move(near_a_d, along_x)

    proj = jnp.concatenate([out_proj, proj_sib], axis=0)
    first_row = lax.axis_index(ALL) * rows
    sib_row = (lax.axis_index(ALL) + sign) * rows
    places = jnp.arange(4, dtype=jnp.int32)
    kinds = jnp.where(places == (x + 1) % 4, 1 - c, c)
    target_table = by_place(targets)
    local_targets = jnp.where(kinds[:, None] == 0, target_table[0], target_table[1])
    local_targets = local_targets.reshape(4, 8, 32).transpose(1, 0, 2).reshape(1, 1024)
    seq_table = by_place(seq_ids).reshape(2, 4, 8, 32).transpose(2, 0, 1, 3).reshape(8, 256)

    hot = hot_rows(jnp.stack([first_row, sib_row]), local_targets, proj.T)

    results = [
        flash(pieces, out_head, head_sib, proj, in_proj)
        for pieces in (
            [hidden],
            [near_a, near_b, near_a_y, near_b_y, near_a_z, near_b_z, far_k, near_a_d],
            [last_y, last_z, far_d],
        )
    ]
    place = jnp.stack(
        [
            k,
            (x + 2 * c) % 4,
            (x - sign + 2 * c + 4) % 4,
            (x - sign + 2 * (1 - c) + 4) % 4,
            (x + 2 + 2 * c) % 4,
        ]
    ).astype(jnp.int32)
    send, side = pack(place, results, hot)
    side_sib = move(side, to_sibling)
    got = lax.all_to_all(send, ALL, 0, 0, tiled=True)
    out = lax.all_to_all(merge(got), ("y", "z"), 0, 0, tiled=True)
    partial = score(kinds.astype(jnp.int32), out, side, side_sib, seq_table, grad_store)
    return finish(lax.all_to_all(partial, ("x", "c"), 0, 0, tiled=True))


def solution(mesh):
    split = Mesh(mesh.devices.reshape(4, 4, 4, 2), ALL)
    everywhere = P(ALL, None)
    return jax.shard_map(
        on_device,
        mesh=split,
        in_specs=(
            P(("x", "c"), None),
            everywhere,
            everywhere,
            P(),
            P(),
            P(),
            P(("y", "z"), ("x", "c")),
        ),
        out_specs=everywhere,
        check_vma=False,
    )
```

```python
import functools

import jax
import jax.numpy as jnp
from jax import lax
from jax.experimental import pallas as pl
from jax.experimental.pallas import tpu as pltpu
from jax.sharding import Mesh
from jax.sharding import PartitionSpec as P

SEQS = 16
ALL = ("y", "z", "x", "c")
TILE = 256
LIMIT = 44 * 1024 * 1024
BF = jnp.bfloat16
F32 = jnp.float32


def index(y, z, x, c):
    return (((y % 4) * 4 + z % 4) * 4 + x % 4) * 2 + c


def move(value, target):
    pairs = [
        (index(y, z, x, c), index(*target(y, z, x, c)))
        for y in range(4)
        for z in range(4)
        for x in range(4)
        for c in range(2)
    ]
    return lax.ppermute(value, ALL, pairs)


def along_x(y, z, x, c):
    return (y, z, x + 1 - 2 * c, c)


def along_x_crossed(y, z, x, c):
    return (y, z, x - 1 + 2 * c, 1 - c)


def along_y(y, z, x, c):
    return (y + 1 - 2 * c, z, x, c)


def along_z(y, z, x, c):
    return (y, z + 1 - 2 * c, x, c)


def to_sibling(y, z, x, c):
    return (y, z, x, 1 - c)


def flash_kernel(sizes, bounds, *refs):
    count = len(sizes)
    pieces, heads = refs[:count], refs[count : count + 2]
    proj_refs, in_ref = refs[count + 2 : count + 4], refs[count + 4]
    out_ref, lse_ref, side_ref = refs[count + 5 : count + 8]
    tok, held, proj, in_proj, scores, piece_sem, head_sem, proj_sem = refs[count + 8 :]
    rows = heads[0].shape[0]

    arrivals = []
    at = 0
    for number, (size, piece) in enumerate(zip(sizes, pieces)):
        arrivals.append(
            pltpu.make_async_copy(piece, tok.at[at : at + size, :], piece_sem.at[number])
        )
        at += size
    blocks = []
    for number, (low, high) in enumerate(zip(bounds, bounds[1:])):
        head, shift = (heads[0], 0) if low < rows else (heads[1], rows)
        blocks.append(
            pltpu.make_async_copy(
                head.at[low - shift : high - shift, :], held.at[low:high, :], head_sem.at[number]
            )
        )
    others = [
        pltpu.make_async_copy(proj_refs[0], proj.at[0:rows, :], proj_sem.at[0]),
        pltpu.make_async_copy(proj_refs[1], proj.at[rows : 2 * rows, :], proj_sem.at[1]),
        pltpu.make_async_copy(in_ref, in_proj, proj_sem.at[2]),
    ]
    for copy in arrivals + blocks + others:
        copy.start()
    for copy in arrivals:
        copy.wait()

    dims = (((1,), (1,)), ((), ()))
    for block, low, high in zip(blocks, bounds, bounds[1:]):
        block.wait()
        scores[:, low:high] = lax.dot_general(
            tok[...], held[low:high, :], dims, preferred_element_type=F32
        )
    for copy in others:
        copy.wait()
    side_ref[...] = jnp.dot(tok[...], in_proj[...], preferred_element_type=F32)

    step = 512
    best = scores[:, 0:step]
    for low in range(step, 2 * rows, step):
        best = jnp.maximum(best, scores[:, low : low + step])
    best = jnp.max(best, axis=1, keepdims=True)
    total = None
    mixed = None
    for low in range(0, 2 * rows, step):
        power = jnp.exp(scores[:, low : low + step] - best)
        total = power if low == 0 else total + power
        part = jnp.dot(
            power.astype(BF), proj[low : low + step, :], preferred_element_type=F32
        )
        mixed = part if low == 0 else mixed + part
    total = jnp.sum(total, axis=1, keepdims=True)
    out_ref[...] = mixed / total
    lse_ref[...] = jnp.broadcast_to(best + jnp.log(total), lse_ref.shape)


def flash(pieces, own, sib, proj_own, proj_sib, in_proj):
    sizes = tuple(p.shape[0] for p in pieces)
    n = sum(sizes)
    rows, depth = own.shape
    rank = proj_own.shape[1]
    bounds = (0, 256, 512, 1024, 1536, 2048)
    here = pl.BlockSpec(memory_space=pltpu.VMEM)
    away = pl.BlockSpec(memory_space=pl.ANY)
    return pl.pallas_call(
        functools.partial(flash_kernel, sizes, bounds),
        in_specs=[away] * (len(pieces) + 5),
        out_specs=[here] * 3,
        out_shape=[jax.ShapeDtypeStruct((n, rank), F32)] * 3,
        scratch_shapes=[
            pltpu.VMEM((n, depth), BF),
            pltpu.VMEM((2 * rows, depth), BF),
            pltpu.VMEM((2 * rows, rank), BF),
            pltpu.VMEM(in_proj.shape, BF),
            pltpu.VMEM((n, 2 * rows), F32),
            pltpu.SemaphoreType.DMA((len(pieces),)),
            pltpu.SemaphoreType.DMA((len(bounds) - 1,)),
            pltpu.SemaphoreType.DMA((3,)),
        ],
        compiler_params=pltpu.CompilerParams(vmem_limit_bytes=LIMIT),
        cost_estimate=pl.CostEstimate(
            flops=2 * n * 2 * rows * depth, bytes_accessed=2 * rows * depth * 2, transcendentals=0
        ),
    )(*pieces, own, sib, proj_own, proj_sib, in_proj)


def hot_kernel(where, targets_ref, own_ref, sib_ref, out_ref):
    local = out_ref.shape[1]
    total = jnp.zeros(out_ref.shape, F32)
    for which, proj_ref in enumerate((own_ref, sib_ref)):
        for first in range(0, proj_ref.shape[0], TILE):
            ids = where[which] + first + lax.broadcasted_iota(jnp.int32, (TILE, local), 0)
            hot = jnp.where(ids == targets_ref[...], 1.0, 0.0).astype(BF)
            total += lax.dot_general(
                proj_ref[first : first + TILE, :],
                hot,
                (((0,), (0,)), ((), ())),
                preferred_element_type=F32,
            )
    out_ref[...] = total


def hot_rows(where, targets, proj_own, proj_sib):
    here = pl.BlockSpec(memory_space=pltpu.VMEM)
    return pl.pallas_call(
        hot_kernel,
        in_specs=[pl.BlockSpec(memory_space=pltpu.SMEM), here, here, here],
        out_specs=here,
        out_shape=jax.ShapeDtypeStruct((proj_own.shape[1], targets.shape[1]), F32),
        compiler_params=pltpu.CompilerParams(vmem_limit_bytes=16 * 1024 * 1024),
        cost_estimate=pl.CostEstimate(
            flops=2 * 128 * 2048 * 1024, bytes_accessed=1 << 20, transcendentals=0
        ),
    )(where, targets, proj_own, proj_sib)


def pack_kernel(place, *refs):
    outs, lses, sides = refs[0:3], refs[3:6], refs[6:9]
    hot_ref, send_ref, side_ref, out_nat, lse_nat = refs[9:]
    k = place[0]
    spot = [place[1], place[2], place[3], place[4]]

    def put(slot, quarter, source, start, rows, into=0):
        for h in range(rows // 32):
            group = quarter * 2 + into + h
            at = slice(start + 32 * h, start + 32 * h + 32)
            out_nat[group, spot[slot]] = outs[source][at, :]
            lse_nat[group, spot[slot]] = lses[source][at, :]
            side_ref[group, spot[slot]] = sides[source][at, :]

    ky, kz, kd = k ^ 2, k ^ 1, k ^ 3
    for q in range(4):
        put(0, q, 0, 64 * q, 64)
    for n, (slot, quarter) in enumerate(
        [(1, k), (2, k), (1, ky), (2, ky), (1, kz), (2, kz), (3, k), (1, kd)]
    ):
        put(slot, quarter, 1, 64 * n, 64)
    put(3, ky, 2, 0, 64)
    put(2, kd, 2, 64, 32)
    put(3, kz, 2, 96, 64)
    put(2, kd, 2, 160, 32, into=1)
    put(3, kd, 2, 192, 64)

    for group in range(8):
        mixed = jnp.transpose(out_nat[group].reshape(128, 128)).reshape(16, 8, 128)
        lse = jnp.transpose(lse_nat[group].reshape(128, 128))[0:8, :]
        high = lse.astype(BF).astype(F32)
        rest = lse - high
        middle = rest.astype(BF).astype(F32)
        low = rest - middle
        line = lax.broadcasted_iota(jnp.int32, (8, 128), 0)
        stats = jnp.where(
            line == 0, high, jnp.where(line == 1, middle, jnp.where(line == 2, low, 0.0))
        )
        hot = hot_ref[:, group * 128 : group * 128 + 128].reshape(16, 8, 128)
        for part in range(16):
            to = (2 * group + part % 2) * 8 + part // 2
            send_ref[to] = jnp.concatenate([mixed[part], hot[part], stats], axis=0).astype(BF)


def pack(place, results, hot):
    outs, lses, sides = zip(*results)
    return pl.pallas_call(
        pack_kernel,
        in_specs=[pl.BlockSpec(memory_space=pltpu.SMEM)]
        + [pl.BlockSpec(memory_space=pltpu.VMEM)] * 10,
        out_specs=[pl.BlockSpec(memory_space=pltpu.VMEM)] * 2,
        out_shape=[
            jax.ShapeDtypeStruct((128, 24, 128), BF),
            jax.ShapeDtypeStruct((8, 4, 32, 128), F32),
        ],
        scratch_shapes=[pltpu.VMEM((8, 4, 32, 128), F32)] * 2,
        compiler_params=pltpu.CompilerParams(vmem_limit_bytes=16 * 1024 * 1024),
    )(place, *outs, *lses, *sides, hot)


def merge_kernel(got_ref, out_ref):
    lse = (
        got_ref[:, 16:24, :].astype(F32)
    )
    lse = lse[:, 0:1, :] + lse[:, 1:2, :] + lse[:, 2:3, :]
    source = lax.broadcasted_iota(jnp.int32, (128, 1, 128), 0)
    lane = lax.broadcasted_iota(jnp.int32, (128, 1, 128), 2)
    x = lax.div(lax.rem(source, 8), 2)
    c = lax.rem(source, 2)
    other = lax.div(lane, 32) == lax.rem(x + 1, 4)
    kind = jnp.where(other, 1 - c, c)
    halves = []
    for which in range(2):
        mine = kind == which
        best = jnp.max(jnp.where(mine, lse, -3.0e38), axis=0, keepdims=True)
        weight = jnp.where(mine, jnp.exp(jnp.minimum(lse - best, 0.0)), 0.0)
        total = jnp.sum(weight, axis=0)
        mixed = jnp.sum(weight * got_ref[:, 0:8, :].astype(F32), axis=0)
        hot = jnp.sum(jnp.where(mine, got_ref[:, 8:16, :].astype(F32), 0.0), axis=0)
        halves.append(mixed / total - hot)
    both = jnp.concatenate(halves, axis=1)
    for copy in range(16):
        out_ref[copy] = both


def merge(got):
    return pl.pallas_call(
        merge_kernel,
        in_specs=[pl.BlockSpec(memory_space=pltpu.VMEM)],
        out_specs=pl.BlockSpec(memory_space=pltpu.VMEM),
        out_shape=jax.ShapeDtypeStruct((16, 8, 256), F32),
        compiler_params=pltpu.CompilerParams(vmem_limit_bytes=16 * 1024 * 1024),
    )(got)


def score_kernel(flags, out_ref, own_ref, sib_ref, seq_ref, store_ref, result_ref, store, sems):
    rows = store.shape[0] // 8
    copies = [
        pltpu.make_async_copy(
            store_ref.at[n * rows : (n + 1) * rows, :],
            store.at[n * rows : (n + 1) * rows, :],
            sems.at[n],
        )
        for n in range(8)
    ]
    for copy in copies:
        copy.start()
    total = jnp.zeros((256, 128), F32)
    for group in range(8):
        out = jnp.concatenate([out_ref[2 * group], out_ref[2 * group + 1]], axis=0)
        ids = seq_ref[group : group + 1, :]
        member = lax.broadcasted_iota(jnp.int32, (16, 256), 0) == ids
        spread = jnp.where(member[None, :, :], out[:, None, :], 0.0).reshape(256, 256)
        first, second = [], []
        for spot in range(4):
            own, sib = own_ref[group, spot], sib_ref[group, spot]
            keep = flags[spot] == 0
            first.append(jnp.where(keep, own, sib))
            second.append(jnp.where(keep, sib, own))
        side = jnp.concatenate(first + second, axis=0)
        spread_high = spread.astype(BF)
        spread_low = (spread - spread_high.astype(F32)).astype(BF)
        side_high = side.astype(BF)
        side_low = (side - side_high.astype(F32)).astype(BF)
        for a, b in (
            (spread_high, side_high),
            (spread_high, side_low),
            (spread_low, side_high),
        ):
            total += jnp.dot(a, b, preferred_element_type=F32)
    grads = jnp.concatenate(
        [total[i * 16 : (i + 1) * 16, :].astype(BF) for i in range(16)], axis=1
    )
    for n, copy in enumerate(copies):
        copy.wait()
        result_ref[n] = lax.dot_general(
            grads,
            store[n * rows : (n + 1) * rows, :],
            (((1,), (1,)), ((), ())),
            preferred_element_type=F32,
        )


def score(flags, out, own, sib, seq, store):
    here = pl.BlockSpec(memory_space=pltpu.VMEM)
    return pl.pallas_call(
        score_kernel,
        in_specs=[
            pl.BlockSpec(memory_space=pltpu.SMEM),
            here,
            here,
            here,
            here,
            pl.BlockSpec(memory_space=pl.ANY),
        ],
        out_specs=here,
        out_shape=jax.ShapeDtypeStruct((8, SEQS, store.shape[0] // 8), F32),
        scratch_shapes=[pltpu.VMEM(store.shape, BF), pltpu.SemaphoreType.DMA((8,))],
        compiler_params=pltpu.CompilerParams(vmem_limit_bytes=50 * 1024 * 1024),
    )(flags, out, own, sib, seq, store)


def finish_kernel(got_ref, out_ref):
    total = got_ref[0]
    for source in range(1, 8):
        total = total + got_ref[source]
    out_ref[...] = total


def finish(got):
    return pl.pallas_call(
        finish_kernel,
        in_specs=[pl.BlockSpec(memory_space=pltpu.VMEM)],
        out_specs=pl.BlockSpec(memory_space=pltpu.VMEM),
        out_shape=jax.ShapeDtypeStruct((SEQS, 256), F32),
    )(got)


def by_place(per_token):
    table = per_token.reshape(4, 2, 256)
    return jnp.stack([table[:, 0], jnp.roll(table[:, 1], 2, axis=0)])


def on_device(hidden, out_head, out_proj, in_proj, targets, seq_ids, grad_store):
    y, z, x, c = (lax.axis_index(name) for name in ALL)
    k = 2 * (y % 2) + z % 2
    sign = 1 - 2 * c
    rows = out_head.shape[0]

    mine = lax.dynamic_slice_in_dim(hidden, k * 64, 64, 0)

    near_a = move(mine, along_x)
    near_b = move(mine, along_x_crossed)
    head_sib = move(out_head, to_sibling)
    proj_sib = move(out_proj, to_sibling)
    again, proj_sib = lax.optimization_barrier((hidden, proj_sib))
    mine_d = lax.dynamic_slice_in_dim(again, (3 - k) * 64, 64, 0)
    mine_d, near_a, head_sib = lax.optimization_barrier((mine_d, near_a, head_sib))
    far_k = move(near_a, along_x)
    near_a_d = move(mine_d, along_x)
    near = jnp.concatenate([near_a, near_b], axis=0)
    near_y = move(near, along_y)
    near_z = move(near, along_z)
    rest = (out_head, head_sib, out_proj, proj_sib, in_proj)
    first = flash([hidden], *rest)
    first, far_k, near_y, near_z = lax.optimization_barrier((first, far_k, near_y, near_z))
    last_y = move(jnp.concatenate([far_k, near_z[64:96]], axis=0), along_y)
    last_z = move(jnp.concatenate([far_k, near_y[96:128]], axis=0), along_z)
    far_d = move(near_a_d, along_x)

    first_row = lax.axis_index(ALL) * rows
    sib_row = (lax.axis_index(ALL) + sign) * rows
    places = jnp.arange(4, dtype=jnp.int32)
    kinds = jnp.where(places == (x + 1) % 4, 1 - c, c)
    target_table = by_place(targets)
    local_targets = jnp.where(kinds[:, None] == 0, target_table[0], target_table[1])
    local_targets = local_targets.reshape(4, 8, 32).transpose(1, 0, 2).reshape(1, 1024)
    seq_table = by_place(seq_ids).reshape(2, 4, 8, 32).transpose(2, 0, 1, 3).reshape(8, 256)

    hot = hot_rows(jnp.stack([first_row, sib_row]), local_targets, out_proj, proj_sib)

    second = flash([near, near_y, near_z, far_k, near_a_d], *rest)
    third = flash([last_y, last_z, far_d], *rest)
    place = jnp.stack(
        [
            k,
            (x + 2 * c) % 4,
            (x - sign + 2 * c + 4) % 4,
            (x - sign + 2 * (1 - c) + 4) % 4,
            (x + 2 + 2 * c) % 4,
        ]
    ).astype(jnp.int32)
    send, side = pack(place, (first, second, third), hot)
    side_sib = move(side, to_sibling)
    got = lax.all_to_all(send, ALL, 0, 0, tiled=True)
    out = lax.all_to_all(merge(got), ("y", "z"), 0, 0, tiled=True)
    partial = score(kinds.astype(jnp.int32), out, side, side_sib, seq_table, grad_store)
    return finish(lax.all_to_all(partial, ("x", "c"), 0, 0, tiled=True)).T


def solution(mesh):
    split = Mesh(mesh.devices.reshape(4, 4, 4, 2), ALL)
    everywhere = P(ALL, None)
    return jax.shard_map(
        on_device,
        mesh=split,
        in_specs=(
            P(("x", "c"), None),
            everywhere,
            everywhere,
            P(),
            P(),
            P(),
            P(("y", "z"), ("x", "c")),
        ),
        out_specs=everywhere,
        check_vma=False,
    )
```

```python
import functools

import jax
import jax.numpy as jnp
from jax import lax
from jax.experimental import pallas as pl
from jax.experimental.pallas import tpu as pltpu
from jax.sharding import Mesh
from jax.sharding import PartitionSpec as P

SEQS = 16
ALL = ("y", "z", "x", "c")
TILE = 256
LIMIT = 26 * 1024 * 1024
BF = jnp.bfloat16
F32 = jnp.float32


def index(y, z, x, c):
    return (((y % 4) * 4 + z % 4) * 4 + x % 4) * 2 + c


def move(value, target):
    pairs = [
        (index(y, z, x, c), index(*target(y, z, x, c)))
        for y in range(4)
        for z in range(4)
        for x in range(4)
        for c in range(2)
    ]
    return lax.ppermute(value, ALL, pairs)


def along_x(y, z, x, c):
    return (y, z, x + 1 - 2 * c, c)


def along_x_crossed(y, z, x, c):
    return (y, z, x - 1 + 2 * c, 1 - c)


def along_y(y, z, x, c):
    return (y + 1 - 2 * c, z, x, c)


def along_z(y, z, x, c):
    return (y, z + 1 - 2 * c, x, c)


def to_sibling(y, z, x, c):
    return (y, z, x, 1 - c)


def rows_kernel(plan, count, *refs):
    where, refs = refs[0], refs[1:]
    sources, results, sems = refs[:count], refs[count:-1], refs[-1]
    copies = []
    for n, (source, start, rows, to, at) in enumerate(plan):
        if isinstance(start, tuple):
            start = pl.multiple_of(where[start[0]] * rows, rows)
        copies.append(
            pltpu.make_async_copy(
                sources[source].at[pl.ds(start, rows), :],
                results[to].at[at : at + rows, :],
                sems.at[n],
            )
        )
    for copy in copies:
        copy.start()
    for copy in copies:
        copy.wait()


def rows_of(plan, where, sources, lengths, limit):
    away = pl.BlockSpec(memory_space=pl.ANY)
    width = sources[0].shape[1]
    return pl.pallas_call(
        functools.partial(rows_kernel, plan, len(sources)),
        in_specs=[pl.BlockSpec(memory_space=pltpu.SMEM)] + [away] * len(sources),
        out_specs=[pl.BlockSpec(memory_space=pl.ANY)] * len(lengths),
        out_shape=[jax.ShapeDtypeStruct((n, width), BF) for n in lengths],
        scratch_shapes=[pltpu.SemaphoreType.DMA((len(plan),))],
        compiler_params=pltpu.CompilerParams(vmem_limit_bytes=limit),
        cost_estimate=pl.CostEstimate(
            flops=0, bytes_accessed=4 * width * sum(lengths), transcendentals=0
        ),
    )(where, *sources)


def flash_kernel(sizes, *refs):
    count = len(sizes)
    pieces, heads = refs[:count], refs[count : count + 2]
    projs, in_ref = refs[count + 2 : count + 4], refs[count + 4]
    out_ref, lse_ref, side_ref = refs[count + 5 : count + 8]
    tok, held, scores, sems, head_sem = refs[count + 8 :]
    rows = heads[0].shape[0]
    chunk = 512

    copies = []
    at = 0
    for number, (size, piece) in enumerate(zip(sizes, pieces)):
        copies.append(pltpu.make_async_copy(piece, tok.at[at : at + size, :], sems.at[number]))
        at += size
    blocks = [
        pltpu.make_async_copy(
            heads[1].at[low : low + chunk, :], held.at[low : low + chunk, :], head_sem.at[n]
        )
        for n, low in enumerate(range(0, rows, chunk))
    ]
    for copy in copies + blocks:
        copy.start()
    for copy in copies:
        copy.wait()

    tile = 1024 if tok.shape[0] <= 256 else 512
    dims = (((1,), (1,)), ((), ()))
    for low in range(0, rows, tile):
        scores[:, low : low + tile] = lax.dot_general(
            tok[...], heads[0][low : low + tile, :], dims, preferred_element_type=F32
        )
    for block in blocks:
        block.wait()
    for low in range(0, rows, tile):
        scores[:, rows + low : rows + low + tile] = lax.dot_general(
            tok[...], held[low : low + tile, :], dims, preferred_element_type=F32
        )
    side_ref[...] = jnp.dot(tok[...], in_ref[...], preferred_element_type=F32)

    step = 512
    best = scores[:, 0:step]
    for low in range(step, 2 * rows, step):
        best = jnp.maximum(best, scores[:, low : low + step])
    best = jnp.max(best, axis=1, keepdims=True)
    total = None
    mixed = None
    for low in range(0, 2 * rows, step):
        power = jnp.exp(scores[:, low : low + step] - best)
        total = power if low == 0 else total + power
        proj = projs[low // rows][low % rows : low % rows + step, :]
        part = jnp.dot(power.astype(BF), proj, preferred_element_type=F32)
        mixed = part if low == 0 else mixed + part
    total = jnp.sum(total, axis=1, keepdims=True)
    out_ref[...] = mixed / total
    lse_ref[...] = jnp.broadcast_to(best + jnp.log(total), lse_ref.shape)


def flash(pieces, own, sib, proj_own, proj_sib, in_proj):
    sizes = tuple(p.shape[0] for p in pieces)
    n = sum(sizes)
    rows, depth = own.shape
    rank = proj_own.shape[1]
    here = pl.BlockSpec(memory_space=pltpu.VMEM)
    away = pl.BlockSpec(memory_space=pl.ANY)
    return pl.pallas_call(
        functools.partial(flash_kernel, sizes),
        in_specs=[away] * len(pieces) + [here, away, here, here, here],
        out_specs=[here] * 3,
        out_shape=[jax.ShapeDtypeStruct((n, rank), F32)] * 3,
        scratch_shapes=[
            pltpu.VMEM((n, depth), BF),
            pltpu.VMEM((rows, depth), BF),
            pltpu.VMEM((n, 2 * rows), F32),
            pltpu.SemaphoreType.DMA((len(pieces),)),
            pltpu.SemaphoreType.DMA((2,)),
        ],
        compiler_params=pltpu.CompilerParams(vmem_limit_bytes=LIMIT),
        cost_estimate=pl.CostEstimate(
            flops=2 * n * 2 * rows * depth, bytes_accessed=n * depth * 2, transcendentals=0
        ),
    )(*pieces, own, sib, proj_own, proj_sib, in_proj)


def hot_kernel(where, targets_ref, own_ref, sib_ref, out_ref):
    local = out_ref.shape[1]
    total = jnp.zeros(out_ref.shape, F32)
    for which, proj_ref in enumerate((own_ref, sib_ref)):
        for first in range(0, proj_ref.shape[0], TILE):
            ids = where[which] + first + lax.broadcasted_iota(jnp.int32, (TILE, local), 0)
            hot = jnp.where(ids == targets_ref[...], 1.0, 0.0).astype(BF)
            total += lax.dot_general(
                proj_ref[first : first + TILE, :],
                hot,
                (((0,), (0,)), ((), ())),
                preferred_element_type=F32,
            )
    out_ref[...] = total


def hot_rows(where, targets, proj_own, proj_sib):
    here = pl.BlockSpec(memory_space=pltpu.VMEM)
    return pl.pallas_call(
        hot_kernel,
        in_specs=[pl.BlockSpec(memory_space=pltpu.SMEM), here, here, here],
        out_specs=here,
        out_shape=jax.ShapeDtypeStruct((proj_own.shape[1], targets.shape[1]), F32),
        compiler_params=pltpu.CompilerParams(vmem_limit_bytes=16 * 1024 * 1024),
        cost_estimate=pl.CostEstimate(
            flops=2 * 128 * 2048 * 1024, bytes_accessed=1 << 20, transcendentals=0
        ),
    )(where, targets, proj_own, proj_sib)


def pack_kernel(place, *refs):
    outs, lses, sides = refs[0:3], refs[3:6], refs[6:9]
    hot_ref, send_ref, side_ref, out_nat, lse_nat = refs[9:]
    k = place[0]
    spot = [place[1], place[2], place[3], place[4]]

    def put(slot, quarter, source, start, rows, into=0):
        for h in range(rows // 32):
            group = quarter * 2 + into + h
            at = slice(start + 32 * h, start + 32 * h + 32)
            out_nat[group, spot[slot]] = outs[source][at, :]
            lse_nat[group, spot[slot]] = lses[source][at, :]
            side_ref[group, spot[slot]] = sides[source][at, :]

    ky, kz, kd = k ^ 2, k ^ 1, k ^ 3
    for q in range(4):
        put(0, q, 0, 64 * q, 64)
    for n, (slot, quarter) in enumerate(
        [(1, k), (2, k), (1, ky), (2, ky), (1, kz), (2, kz), (3, k), (1, kd)]
    ):
        put(slot, quarter, 1, 64 * n, 64)
    put(3, ky, 2, 0, 64)
    put(2, kd, 2, 64, 32)
    put(3, kz, 2, 96, 64)
    put(2, kd, 2, 160, 32, into=1)
    put(3, kd, 2, 192, 64)

    for group in range(8):
        mixed = jnp.transpose(out_nat[group].reshape(128, 128)).reshape(16, 8, 128)
        lse = jnp.transpose(lse_nat[group].reshape(128, 128))[0:8, :]
        high = lse.astype(BF).astype(F32)
        rest = lse - high
        middle = rest.astype(BF).astype(F32)
        low = rest - middle
        line = lax.broadcasted_iota(jnp.int32, (8, 128), 0)
        stats = jnp.where(
            line == 0, high, jnp.where(line == 1, middle, jnp.where(line == 2, low, 0.0))
        )
        hot = hot_ref[:, group * 128 : group * 128 + 128].reshape(16, 8, 128)
        for part in range(16):
            to = (2 * group + part % 2) * 8 + part // 2
            send_ref[to] = jnp.concatenate([mixed[part], hot[part], stats], axis=0).astype(BF)


def pack(place, results, hot):
    outs, lses, sides = zip(*results)
    return pl.pallas_call(
        pack_kernel,
        in_specs=[pl.BlockSpec(memory_space=pltpu.SMEM)]
        + [pl.BlockSpec(memory_space=pltpu.VMEM)] * 10,
        out_specs=[pl.BlockSpec(memory_space=pltpu.VMEM)] * 2,
        out_shape=[
            jax.ShapeDtypeStruct((128, 24, 128), BF),
            jax.ShapeDtypeStruct((8, 4, 32, 128), F32),
        ],
        scratch_shapes=[pltpu.VMEM((8, 4, 32, 128), F32)] * 2,
        compiler_params=pltpu.CompilerParams(vmem_limit_bytes=16 * 1024 * 1024),
    )(place, *outs, *lses, *sides, hot)


def merge_kernel(got_ref, out_ref):
    lse = (
        got_ref[:, 16:24, :].astype(F32)
    )
    lse = lse[:, 0:1, :] + lse[:, 1:2, :] + lse[:, 2:3, :]
    source = lax.broadcasted_iota(jnp.int32, (128, 1, 128), 0)
    lane = lax.broadcasted_iota(jnp.int32, (128, 1, 128), 2)
    x = lax.div(lax.rem(source, 8), 2)
    c = lax.rem(source, 2)
    other = lax.div(lane, 32) == lax.rem(x + 1, 4)
    kind = jnp.where(other, 1 - c, c)
    halves = []
    for which in range(2):
        mine = kind == which
        best = jnp.max(jnp.where(mine, lse, -3.0e38), axis=0, keepdims=True)
        weight = jnp.where(mine, jnp.exp(jnp.minimum(lse - best, 0.0)), 0.0)
        total = jnp.sum(weight, axis=0)
        mixed = jnp.sum(weight * got_ref[:, 0:8, :].astype(F32), axis=0)
        hot = jnp.sum(jnp.where(mine, got_ref[:, 8:16, :].astype(F32), 0.0), axis=0)
        halves.append(mixed / total - hot)
    both = jnp.concatenate(halves, axis=1)
    for copy in range(16):
        out_ref[copy] = both


def merge(got):
    return pl.pallas_call(
        merge_kernel,
        in_specs=[pl.BlockSpec(memory_space=pltpu.VMEM)],
        out_specs=pl.BlockSpec(memory_space=pltpu.VMEM),
        out_shape=jax.ShapeDtypeStruct((16, 8, 256), F32),
        compiler_params=pltpu.CompilerParams(vmem_limit_bytes=16 * 1024 * 1024),
    )(got)


def score_kernel(flags, out_ref, own_ref, sib_ref, seq_ref, store_ref, result_ref, store, sems):
    rows = store.shape[0] // 8
    copies = [
        pltpu.make_async_copy(
            store_ref.at[n * rows : (n + 1) * rows, :],
            store.at[n * rows : (n + 1) * rows, :],
            sems.at[n],
        )
        for n in range(8)
    ]
    for copy in copies:
        copy.start()
    total = jnp.zeros((256, 128), F32)
    for group in range(8):
        out = jnp.concatenate([out_ref[2 * group], out_ref[2 * group + 1]], axis=0)
        ids = seq_ref[group : group + 1, :]
        member = lax.broadcasted_iota(jnp.int32, (16, 256), 0) == ids
        spread = jnp.where(member[None, :, :], out[:, None, :], 0.0).reshape(256, 256)
        first, second = [], []
        for spot in range(4):
            own, sib = own_ref[group, spot], sib_ref[group, spot]
            keep = flags[spot] == 0
            first.append(jnp.where(keep, own, sib))
            second.append(jnp.where(keep, sib, own))
        side = jnp.concatenate(first + second, axis=0)
        spread_high = spread.astype(BF)
        spread_low = (spread - spread_high.astype(F32)).astype(BF)
        side_high = side.astype(BF)
        side_low = (side - side_high.astype(F32)).astype(BF)
        for a, b in (
            (spread_high, side_high),
            (spread_high, side_low),
            (spread_low, side_high),
        ):
            total += jnp.dot(a, b, preferred_element_type=F32)
    grads = jnp.concatenate(
        [total[i * 16 : (i + 1) * 16, :].astype(BF) for i in range(16)], axis=1
    )
    for n, copy in enumerate(copies):
        copy.wait()
        result_ref[n] = lax.dot_general(
            grads,
            store[n * rows : (n + 1) * rows, :],
            (((1,), (1,)), ((), ())),
            preferred_element_type=F32,
        )


def score(flags, out, own, sib, seq, store):
    here = pl.BlockSpec(memory_space=pltpu.VMEM)
    return pl.pallas_call(
        score_kernel,
        in_specs=[
            pl.BlockSpec(memory_space=pltpu.SMEM),
            here,
            here,
            here,
            here,
            pl.BlockSpec(memory_space=pl.ANY),
        ],
        out_specs=here,
        out_shape=jax.ShapeDtypeStruct((8, SEQS, store.shape[0] // 8), F32),
        scratch_shapes=[pltpu.VMEM(store.shape, BF), pltpu.SemaphoreType.DMA((8,))],
        compiler_params=pltpu.CompilerParams(vmem_limit_bytes=48 * 1024 * 1024),
    )(flags, out, own, sib, seq, store)


def by_place(per_token):
    table = per_token.reshape(4, 2, 256)
    return jnp.stack([table[:, 0], jnp.roll(table[:, 1], 2, axis=0)])


def on_device(hidden, out_head, out_proj, in_proj, targets, seq_ids, grad_store):
    y, z, x, c = (lax.axis_index(name) for name in ALL)
    k = 2 * (y % 2) + z % 2
    sign = 1 - 2 * c
    rows = out_head.shape[0]

    quarters = jnp.stack([k, 3 - k]).astype(jnp.int32)

    mine, mine_d = rows_of(
        ((0, (0,), 64, 0, 0), (0, (1,), 64, 1, 0)), quarters, [hidden], [64, 64], 60 << 20
    )
    near_a = move(mine, along_x)
    near_b = move(mine, along_x_crossed)
    head_sib = move(out_head, to_sibling)
    proj_sib = move(out_proj, to_sibling)
    mine_d, near_a, head_sib = lax.optimization_barrier((mine_d, near_a, head_sib))
    far_k = move(near_a, along_x)
    near_a_d = move(mine_d, along_x)
    near = rows_of(((0, 0, 64, 0, 0), (1, 0, 64, 0, 64)), quarters, [near_a, near_b], [128], 16 << 20)[0]
    near_y = move(near, along_y)
    near_z = move(near, along_z)

    rest = (out_head, head_sib, out_proj, proj_sib, in_proj)
    first = flash([hidden], *rest)
    first, far_k, near_y, near_z = lax.optimization_barrier((first, far_k, near_y, near_z))
    last_y, last_z = rows_of(
        ((0, 0, 64, 0, 0), (2, 64, 32, 0, 64), (0, 0, 64, 1, 0), (1, 96, 32, 1, 64)),
        quarters,
        [far_k, near_y, near_z],
        [96, 96],
        16 << 20,
    )
    last_y = move(last_y, along_y)
    last_z = move(last_z, along_z)
    far_d = move(near_a_d, along_x)

    first_row = lax.axis_index(ALL) * rows
    sib_row = (lax.axis_index(ALL) + sign) * rows
    places = jnp.arange(4, dtype=jnp.int32)
    kinds = jnp.where(places == (x + 1) % 4, 1 - c, c)
    target_table = by_place(targets)
    local_targets = jnp.where(kinds[:, None] == 0, target_table[0], target_table[1])
    local_targets = local_targets.reshape(4, 8, 32).transpose(1, 0, 2).reshape(1, 1024)
    seq_table = by_place(seq_ids).reshape(2, 4, 8, 32).transpose(2, 0, 1, 3).reshape(8, 256)

    hot = hot_rows(jnp.stack([first_row, sib_row]), local_targets, out_proj, proj_sib)

    second = flash([near, near_y, near_z, far_k, near_a_d], *rest)
    third = flash([last_y, last_z, far_d], *rest)
    place = jnp.stack(
        [
            k,
            (x + 2 * c) % 4,
            (x - sign + 2 * c + 4) % 4,
            (x - sign + 2 * (1 - c) + 4) % 4,
            (x + 2 + 2 * c) % 4,
        ]
    ).astype(jnp.int32)
    send, side = pack(place, (first, second, third), hot)
    side_sib = move(side, to_sibling)

    got = lax.all_to_all(send, ALL, 0, 0, tiled=True)

    out = lax.all_to_all(merge(got), ("y", "z"), 0, 0, tiled=True)
    partial = score(kinds.astype(jnp.int32), out, side, side_sib, seq_table, grad_store)
    return jnp.sum(lax.all_to_all(partial, ("x", "c"), 0, 0, tiled=True), axis=0).T


def solution(mesh):
    split = Mesh(mesh.devices.reshape(4, 4, 4, 2), ALL)
    everywhere = P(ALL, None)
    return jax.shard_map(
        on_device,
        mesh=split,
        in_specs=(
            P(("x", "c"), None),
            everywhere,
            everywhere,
            P(),
            P(),
            P(),
            P(("y", "z"), ("x", "c")),
        ),
        out_specs=everywhere,
        check_vma=False,
    )
```

```python
import functools

import jax
import jax.numpy as jnp
from jax import lax
from jax.experimental import pallas as pl
from jax.experimental.pallas import tpu as pltpu
from jax.sharding import Mesh
from jax.sharding import PartitionSpec as P

SEQS = 16
ALL = ("y", "z", "x", "c")
TILE = 256
LIMIT = 26 * 1024 * 1024
BF = jnp.bfloat16
F32 = jnp.float32


def index(y, z, x, c):
    return (((y % 4) * 4 + z % 4) * 4 + x % 4) * 2 + c


def move(value, target):
    pairs = [
        (index(y, z, x, c), index(*target(y, z, x, c)))
        for y in range(4)
        for z in range(4)
        for x in range(4)
        for c in range(2)
    ]
    return lax.ppermute(value, ALL, pairs)


def along_x(y, z, x, c):
    return (y, z, x + 1 - 2 * c, c)


def along_x_crossed(y, z, x, c):
    return (y, z, x - 1 + 2 * c, 1 - c)


def along_y(y, z, x, c):
    return (y + 1 - 2 * c, z, x, c)


def along_z(y, z, x, c):
    return (y, z + 1 - 2 * c, x, c)


def to_sibling(y, z, x, c):
    return (y, z, x, 1 - c)


def rows_kernel(plan, count, *refs):
    where, refs = refs[0], refs[1:]
    sources, results, sems = refs[:count], refs[count:-1], refs[-1]
    copies = []
    for n, (source, start, rows, to, at) in enumerate(plan):
        if isinstance(start, tuple):
            start = pl.multiple_of(where[start[0]] * rows, rows)
        copies.append(
            pltpu.make_async_copy(
                sources[source].at[pl.ds(start, rows), :],
                results[to].at[at : at + rows, :],
                sems.at[n],
            )
        )
    for copy in copies:
        copy.start()
    for copy in copies:
        copy.wait()


def rows_of(plan, where, sources, lengths, limit, space=pl.ANY):
    away = pl.BlockSpec(memory_space=pl.ANY)
    width = sources[0].shape[1]
    return pl.pallas_call(
        functools.partial(rows_kernel, plan, len(sources)),
        in_specs=[pl.BlockSpec(memory_space=pltpu.SMEM)] + [away] * len(sources),
        out_specs=[pl.BlockSpec(memory_space=space)] * len(lengths),
        out_shape=[jax.ShapeDtypeStruct((n, width), BF) for n in lengths],
        scratch_shapes=[pltpu.SemaphoreType.DMA((len(plan),))],
        compiler_params=pltpu.CompilerParams(vmem_limit_bytes=limit),
        cost_estimate=pl.CostEstimate(
            flops=0, bytes_accessed=4 * width * sum(lengths), transcendentals=0
        ),
    )(where, *sources)


def flash_kernel(sizes, stream, *refs):
    count = len(sizes)
    pieces, heads = refs[:count], refs[count : count + 2]
    projs, in_ref = refs[count + 2 : count + 4], refs[count + 4]
    out_ref, lse_ref, side_ref = refs[count + 5 : count + 8]
    tok, held, scores, sems, head_sem = refs[count + 8 : count + 13]
    rows = heads[0].shape[0]
    chunk = 512

    copies = []
    at = 0
    for number, (size, piece) in enumerate(zip(sizes, pieces)):
        copies.append(pltpu.make_async_copy(piece, tok.at[at : at + size, :], sems.at[number]))
        at += size
    blocks = []
    for head in heads if stream else heads[1:]:
        for low in range(0, rows, chunk):
            at = len(blocks)
            blocks.append(
                pltpu.make_async_copy(
                    head.at[low : low + chunk, :],
                    held.at[at * chunk : (at + 1) * chunk, :],
                    head_sem.at[at],
                )
            )
    others = []
    if stream:
        far = (*projs, in_ref)
        *projs, in_ref = refs[count + 13 : count + 16]
        for n, (source, target) in enumerate(zip(far, (*projs, in_ref))):
            others.append(pltpu.make_async_copy(source, target, refs[count + 16].at[n]))
    for copy in copies + blocks[:2] + others:
        copy.start()
    for copy in copies:
        copy.wait()

    dims = (((1,), (1,)), ((), ()))
    tile = 1024 if tok.shape[0] <= 256 else 512
    if not stream:
        for low in range(0, rows, tile):
            scores[:, low : low + tile] = lax.dot_general(
                tok[...], heads[0][low : low + tile, :], dims, preferred_element_type=F32
            )
        for block in blocks:
            block.wait()
        for low in range(0, rows, tile):
            scores[:, rows + low : rows + low + tile] = lax.dot_general(
                tok[...], held[low : low + tile, :], dims, preferred_element_type=F32
            )
    else:
        for n, block in enumerate(blocks):
            block.wait()
            if n + 2 < len(blocks):
                blocks[n + 2].start()
            low = n * chunk
            scores[:, low : low + chunk] = lax.dot_general(
                tok[...], held[low : low + chunk, :], dims, preferred_element_type=F32
            )
    for copy in others:
        copy.wait()
    side_ref[...] = jnp.dot(tok[...], in_ref[...], preferred_element_type=F32)

    step = 512
    best = scores[:, 0:step]
    for low in range(step, 2 * rows, step):
        best = jnp.maximum(best, scores[:, low : low + step])
    best = jnp.max(best, axis=1, keepdims=True)
    total = None
    mixed = None
    for low in range(0, 2 * rows, step):
        power = jnp.exp(scores[:, low : low + step] - best)
        total = power if low == 0 else total + power
        proj = projs[low // rows][low % rows : low % rows + step, :]
        part = jnp.dot(power.astype(BF), proj, preferred_element_type=F32)
        mixed = part if low == 0 else mixed + part
    total = jnp.sum(total, axis=1, keepdims=True)
    out_ref[...] = mixed / total
    lse_ref[...] = jnp.broadcast_to(best + jnp.log(total), lse_ref.shape)


def flash(pieces, own, sib, proj_own, proj_sib, in_proj, stream=False):
    sizes = tuple(p.shape[0] for p in pieces)
    n = sum(sizes)
    rows, depth = own.shape
    rank = proj_own.shape[1]
    here = pl.BlockSpec(memory_space=pltpu.VMEM)
    away = pl.BlockSpec(memory_space=pl.ANY)
    extra = []
    if stream:
        extra = [pltpu.VMEM(a.shape, BF) for a in (proj_own, proj_sib, in_proj)]
        extra.append(pltpu.SemaphoreType.DMA((3,)))
    return pl.pallas_call(
        functools.partial(flash_kernel, sizes, stream),
        in_specs=[away] * len(pieces) + ([away] * 5 if stream else [here, away, here, here, here]),
        out_specs=[here] * 3,
        out_shape=[jax.ShapeDtypeStruct((n, rank), F32)] * 3,
        scratch_shapes=[
            pltpu.VMEM((n, depth), BF),
            pltpu.VMEM((2 * rows if stream else rows, depth), BF),
            pltpu.VMEM((n, 2 * rows), F32),
            pltpu.SemaphoreType.DMA((len(pieces),)),
            pltpu.SemaphoreType.DMA((4 if stream else 2,)),
        ]
        + extra,
        compiler_params=pltpu.CompilerParams(vmem_limit_bytes=(44 << 20) if stream else LIMIT),
        cost_estimate=pl.CostEstimate(
            flops=2 * n * 2 * rows * depth, bytes_accessed=n * depth * 2, transcendentals=0
        ),
    )(*pieces, own, sib, proj_own, proj_sib, in_proj)


def hot_kernel(where, targets_ref, own_ref, sib_ref, out_ref):
    local = out_ref.shape[1]
    total = jnp.zeros(out_ref.shape, F32)
    for which, proj_ref in enumerate((own_ref, sib_ref)):
        for first in range(0, proj_ref.shape[0], TILE):
            ids = where[which] + first + lax.broadcasted_iota(jnp.int32, (TILE, local), 0)
            hot = jnp.where(ids == targets_ref[...], 1.0, 0.0).astype(BF)
            total += lax.dot_general(
                proj_ref[first : first + TILE, :],
                hot,
                (((0,), (0,)), ((), ())),
                preferred_element_type=F32,
            )
    out_ref[...] = total


def hot_rows(where, targets, proj_own, proj_sib):
    here = pl.BlockSpec(memory_space=pltpu.VMEM)
    return pl.pallas_call(
        hot_kernel,
        in_specs=[pl.BlockSpec(memory_space=pltpu.SMEM), here, here, here],
        out_specs=here,
        out_shape=jax.ShapeDtypeStruct((proj_own.shape[1], targets.shape[1]), F32),
        compiler_params=pltpu.CompilerParams(vmem_limit_bytes=16 * 1024 * 1024),
        cost_estimate=pl.CostEstimate(
            flops=2 * 128 * 2048 * 1024, bytes_accessed=1 << 20, transcendentals=0
        ),
    )(where, targets, proj_own, proj_sib)


def pack_kernel(place, *refs):
    outs, lses, sides = refs[0:3], refs[3:6], refs[6:9]
    hot_ref, send_ref, side_ref, out_nat, lse_nat = refs[9:]
    k = place[0]
    spot = [place[1], place[2], place[3], place[4]]

    def put(slot, quarter, source, start, rows, into=0):
        for h in range(rows // 32):
            group = quarter * 2 + into + h
            at = slice(start + 32 * h, start + 32 * h + 32)
            out_nat[group, spot[slot]] = outs[source][at, :]
            lse_nat[group, spot[slot]] = lses[source][at, :]
            side_ref[group, spot[slot]] = sides[source][at, :]

    ky, kz, kd = k ^ 2, k ^ 1, k ^ 3
    for q in range(4):
        put(0, q, 0, 64 * q, 64)
    for n, (slot, quarter) in enumerate(
        [(1, k), (2, k), (1, ky), (2, ky), (1, kz), (2, kz), (3, k), (1, kd)]
    ):
        put(slot, quarter, 1, 64 * n, 64)
    put(3, ky, 2, 0, 64)
    put(2, kd, 2, 64, 32)
    put(3, kz, 2, 96, 64)
    put(2, kd, 2, 160, 32, into=1)
    put(3, kd, 2, 192, 64)

    for group in range(8):
        mixed = jnp.transpose(out_nat[group].reshape(128, 128)).reshape(16, 8, 128)
        lse = jnp.transpose(lse_nat[group].reshape(128, 128))[0:8, :]
        high = lse.astype(BF).astype(F32)
        rest = lse - high
        middle = rest.astype(BF).astype(F32)
        low = rest - middle
        line = lax.broadcasted_iota(jnp.int32, (8, 128), 0)
        stats = jnp.where(
            line == 0, high, jnp.where(line == 1, middle, jnp.where(line == 2, low, 0.0))
        )
        hot = hot_ref[:, group * 128 : group * 128 + 128].reshape(16, 8, 128)
        for part in range(16):
            to = (2 * group + part % 2) * 8 + part // 2
            send_ref[to] = jnp.concatenate([mixed[part], hot[part], stats], axis=0).astype(BF)


def pack(place, results, hot):
    outs, lses, sides = zip(*results)
    return pl.pallas_call(
        pack_kernel,
        in_specs=[pl.BlockSpec(memory_space=pltpu.SMEM)]
        + [pl.BlockSpec(memory_space=pltpu.VMEM)] * 10,
        out_specs=[pl.BlockSpec(memory_space=pltpu.VMEM)] * 2,
        out_shape=[
            jax.ShapeDtypeStruct((128, 24, 128), BF),
            jax.ShapeDtypeStruct((8, 4, 32, 128), F32),
        ],
        scratch_shapes=[pltpu.VMEM((8, 4, 32, 128), F32)] * 2,
        compiler_params=pltpu.CompilerParams(vmem_limit_bytes=16 * 1024 * 1024),
    )(place, *outs, *lses, *sides, hot)


def merge_kernel(got_ref, out_ref):
    lse = (
        got_ref[:, 16:24, :].astype(F32)
    )
    lse = lse[:, 0:1, :] + lse[:, 1:2, :] + lse[:, 2:3, :]
    source = lax.broadcasted_iota(jnp.int32, (128, 1, 128), 0)
    lane = lax.broadcasted_iota(jnp.int32, (128, 1, 128), 2)
    x = lax.div(lax.rem(source, 8), 2)
    c = lax.rem(source, 2)
    other = lax.div(lane, 32) == lax.rem(x + 1, 4)
    kind = jnp.where(other, 1 - c, c)
    halves = []
    for which in range(2):
        mine = kind == which
        best = jnp.max(jnp.where(mine, lse, -3.0e38), axis=0, keepdims=True)
        weight = jnp.where(mine, jnp.exp(jnp.minimum(lse - best, 0.0)), 0.0)
        total = jnp.sum(weight, axis=0)
        mixed = jnp.sum(weight * got_ref[:, 0:8, :].astype(F32), axis=0)
        hot = jnp.sum(jnp.where(mine, got_ref[:, 8:16, :].astype(F32), 0.0), axis=0)
        halves.append(mixed / total - hot)
    both = jnp.concatenate(halves, axis=1)
    for copy in range(16):
        out_ref[copy] = both


def merge(got):
    return pl.pallas_call(
        merge_kernel,
        in_specs=[pl.BlockSpec(memory_space=pltpu.VMEM)],
        out_specs=pl.BlockSpec(memory_space=pltpu.VMEM),
        out_shape=jax.ShapeDtypeStruct((16, 8, 256), F32),
        compiler_params=pltpu.CompilerParams(vmem_limit_bytes=16 * 1024 * 1024),
    )(got)


def score_kernel(
    flags, out_ref, own_hbm, sib_hbm, seq_ref, store_ref, result_ref, own_ref, sib_ref, store, sems, side_sem
):
    rows = store.shape[0] // 8
    copies = [
        pltpu.make_async_copy(
            store_ref.at[n * rows : (n + 1) * rows, :],
            store.at[n * rows : (n + 1) * rows, :],
            sems.at[n],
        )
        for n in range(8)
    ]
    sides = [
        pltpu.make_async_copy(own_hbm, own_ref, side_sem.at[0]),
        pltpu.make_async_copy(sib_hbm, sib_ref, side_sem.at[1]),
    ]
    for copy in sides + copies[:3]:
        copy.start()
    for copy in sides:
        copy.wait()
    total = jnp.zeros((256, 128), F32)
    for group in range(8):
        out = jnp.concatenate([out_ref[2 * group], out_ref[2 * group + 1]], axis=0)
        ids = seq_ref[group : group + 1, :]
        member = lax.broadcasted_iota(jnp.int32, (16, 256), 0) == ids
        spread = jnp.where(member[None, :, :], out[:, None, :], 0.0).reshape(256, 256)
        first, second = [], []
        for spot in range(4):
            own, sib = own_ref[group, spot], sib_ref[group, spot]
            keep = flags[spot] == 0
            first.append(jnp.where(keep, own, sib))
            second.append(jnp.where(keep, sib, own))
        side = jnp.concatenate(first + second, axis=0)
        spread_high = spread.astype(BF)
        spread_low = (spread - spread_high.astype(F32)).astype(BF)
        side_high = side.astype(BF)
        side_low = (side - side_high.astype(F32)).astype(BF)
        for a, b in (
            (spread_high, side_high),
            (spread_high, side_low),
            (spread_low, side_high),
        ):
            total += jnp.dot(a, b, preferred_element_type=F32)
    grads = jnp.concatenate(
        [total[i * 16 : (i + 1) * 16, :].astype(BF) for i in range(16)], axis=1
    )
    for n, copy in enumerate(copies):
        copy.wait()
        if n + 3 < 8:
            copies[n + 3].start()
        result_ref[n] = lax.dot_general(
            grads,
            store[n * rows : (n + 1) * rows, :],
            (((1,), (1,)), ((), ())),
            preferred_element_type=F32,
        )


def score(flags, out, own, sib, seq, store):
    here = pl.BlockSpec(memory_space=pltpu.VMEM)
    away = pl.BlockSpec(memory_space=pl.ANY)
    return pl.pallas_call(
        score_kernel,
        in_specs=[
            pl.BlockSpec(memory_space=pltpu.SMEM),
            here,
            away,
            away,
            here,
            away,
        ],
        out_specs=here,
        out_shape=jax.ShapeDtypeStruct((8, SEQS, store.shape[0] // 8), F32),
        scratch_shapes=[
            pltpu.VMEM(own.shape, F32),
            pltpu.VMEM(own.shape, F32),
            pltpu.VMEM(store.shape, BF),
            pltpu.SemaphoreType.DMA((8,)),
            pltpu.SemaphoreType.DMA((2,)),
        ],
        compiler_params=pltpu.CompilerParams(vmem_limit_bytes=48 * 1024 * 1024),
    )(flags, out, own, sib, seq, store)


def by_place(per_token):
    table = per_token.reshape(4, 2, 256)
    return jnp.stack([table[:, 0], jnp.roll(table[:, 1], 2, axis=0)])


def on_device(hidden, out_head, out_proj, in_proj, targets, seq_ids, grad_store):
    y, z, x, c = (lax.axis_index(name) for name in ALL)
    k = 2 * (y % 2) + z % 2
    sign = 1 - 2 * c
    rows = out_head.shape[0]

    quarters = jnp.stack([k, 3 - k]).astype(jnp.int32)

    mine, mine_d = rows_of(
        ((0, (0,), 64, 0, 0), (0, (1,), 64, 1, 0)), quarters, [hidden], [64, 64], 58 << 20, pltpu.VMEM
    )
    near_a = move(mine, along_x)
    near_b = move(mine, along_x_crossed)
    head_sib = move(out_head, to_sibling)
    proj_sib = move(out_proj, to_sibling)
    mine_d, near_a, head_sib = lax.optimization_barrier((mine_d, near_a, head_sib))
    far_k = move(near_a, along_x)
    near_a_d = move(mine_d, along_x)
    near = rows_of(((0, 0, 64, 0, 0), (1, 0, 64, 0, 64)), quarters, [near_a, near_b], [128], 16 << 20)[0]
    near_y = move(near, along_y)
    near_z = move(near, along_z)

    rest = (out_head, head_sib, out_proj, proj_sib, in_proj)
    first = flash([hidden], *rest, stream=True)
    first, far_k, near_y, near_z = lax.optimization_barrier((first, far_k, near_y, near_z))
    last_y, last_z = rows_of(
        ((0, 0, 64, 0, 0), (2, 64, 32, 0, 64), (0, 0, 64, 1, 0), (1, 96, 32, 1, 64)),
        quarters,
        [far_k, near_y, near_z],
        [96, 96],
        16 << 20,
    )
    last_y = move(last_y, along_y)
    last_z = move(last_z, along_z)
    far_d = move(near_a_d, along_x)

    first_row = lax.axis_index(ALL) * rows
    sib_row = (lax.axis_index(ALL) + sign) * rows
    places = jnp.arange(4, dtype=jnp.int32)
    kinds = jnp.where(places == (x + 1) % 4, 1 - c, c)
    target_table = by_place(targets)
    local_targets = jnp.where(kinds[:, None] == 0, target_table[0], target_table[1])
    local_targets = local_targets.reshape(4, 8, 32).transpose(1, 0, 2).reshape(1, 1024)
    seq_table = by_place(seq_ids).reshape(2, 4, 8, 32).transpose(2, 0, 1, 3).reshape(8, 256)

    hot = hot_rows(jnp.stack([first_row, sib_row]), local_targets, out_proj, proj_sib)

    second = flash([near, near_y, near_z, far_k, near_a_d], *rest)
    third = flash([last_y, last_z, far_d], *rest)
    place = jnp.stack(
        [
            k,
            (x + 2 * c) % 4,
            (x - sign + 2 * c + 4) % 4,
            (x - sign + 2 * (1 - c) + 4) % 4,
            (x + 2 + 2 * c) % 4,
        ]
    ).astype(jnp.int32)
    send, side = pack(place, (first, second, third), hot)
    side_sib = move(side, to_sibling)

    got = lax.all_to_all(send, ALL, 0, 0, tiled=True)

    out = lax.all_to_all(merge(got), ("y", "z"), 0, 0, tiled=True)
    partial = score(kinds.astype(jnp.int32), out, side, side_sib, seq_table, grad_store)
    return jnp.sum(lax.all_to_all(partial, ("x", "c"), 0, 0, tiled=True), axis=0).T


def solution(mesh):
    split = Mesh(mesh.devices.reshape(4, 4, 4, 2), ALL)
    everywhere = P(ALL, None)
    return jax.shard_map(
        on_device,
        mesh=split,
        in_specs=(
            P(("x", "c"), None),
            everywhere,
            everywhere,
            P(),
            P(),
            P(),
            P(("y", "z"), ("x", "c")),
        ),
        out_specs=everywhere,
        check_vma=False,
    )
```

```python
import functools

import jax
import jax.numpy as jnp
from jax import lax
from jax.experimental import pallas as pl
from jax.experimental.pallas import tpu as pltpu
from jax.sharding import Mesh
from jax.sharding import PartitionSpec as P

SEQS = 16
ALL = ("y", "z", "x", "c")
TILE = 256
LIMIT = 26 * 1024 * 1024
BF = jnp.bfloat16
F32 = jnp.float32


def index(y, z, x, c):
    return (((y % 4) * 4 + z % 4) * 4 + x % 4) * 2 + c


def move(value, target):
    pairs = [
        (index(y, z, x, c), index(*target(y, z, x, c)))
        for y in range(4)
        for z in range(4)
        for x in range(4)
        for c in range(2)
    ]
    return lax.ppermute(value, ALL, pairs)


def along_x(y, z, x, c):
    return (y, z, x + 1 - 2 * c, c)


def along_x_crossed(y, z, x, c):
    return (y, z, x - 1 + 2 * c, 1 - c)


def along_y(y, z, x, c):
    return (y + 1 - 2 * c, z, x, c)


def along_z(y, z, x, c):
    return (y, z + 1 - 2 * c, x, c)


def to_sibling(y, z, x, c):
    return (y, z, x, 1 - c)


def rows_kernel(plan, count, *refs):
    sources, results, sems = refs[:count], refs[count:-1], refs[-1]
    copies = [
        pltpu.make_async_copy(
            sources[source].at[start : start + rows, :],
            results[to].at[at : at + rows, :],
            sems.at[n],
        )
        for n, (source, start, rows, to, at) in enumerate(plan)
    ]
    for copy in copies:
        copy.start()
    for copy in copies:
        copy.wait()


def rows_of(plan, sources, lengths):
    away = pl.BlockSpec(memory_space=pl.ANY)
    width = sources[0].shape[1]
    return pl.pallas_call(
        functools.partial(rows_kernel, plan, len(sources)),
        in_specs=[away] * len(sources),
        out_specs=[away] * len(lengths),
        out_shape=[jax.ShapeDtypeStruct((n, width), BF) for n in lengths],
        scratch_shapes=[pltpu.SemaphoreType.DMA((len(plan),))],
        compiler_params=pltpu.CompilerParams(vmem_limit_bytes=16 * 1024 * 1024),
        cost_estimate=pl.CostEstimate(
            flops=0, bytes_accessed=4 * width * sum(lengths), transcendentals=0
        ),
    )(*sources)


def flash_kernel(sizes, stream, *refs):
    count = len(sizes)
    pieces, heads = refs[:count], refs[count : count + 2]
    projs, in_ref = refs[count + 2 : count + 4], refs[count + 4]
    out_ref, lse_ref, side_ref = refs[count + 5 : count + 8]
    tok, held, scores, sems, head_sem = refs[count + 8 : count + 13]
    rows = heads[0].shape[0]
    chunk = 512

    copies = []
    at = 0
    for number, (size, piece) in enumerate(zip(sizes, pieces)):
        copies.append(pltpu.make_async_copy(piece, tok.at[at : at + size, :], sems.at[number]))
        at += size
    blocks = []
    for head in heads if stream else heads[1:]:
        for low in range(0, rows, chunk):
            at = len(blocks)
            blocks.append(
                pltpu.make_async_copy(
                    head.at[low : low + chunk, :],
                    held.at[at * chunk : (at + 1) * chunk, :],
                    head_sem.at[at],
                )
            )
    others = []
    if stream:
        far = (*projs, in_ref)
        *projs, in_ref = refs[count + 13 : count + 16]
        for n, (source, target) in enumerate(zip(far, (*projs, in_ref))):
            others.append(pltpu.make_async_copy(source, target, refs[count + 16].at[n]))
    for copy in copies + blocks[:2] + others:
        copy.start()
    for copy in copies:
        copy.wait()

    dims = (((1,), (1,)), ((), ()))
    tile = 1024 if tok.shape[0] <= 256 else 512
    if not stream:
        for low in range(0, rows, tile):
            scores[:, low : low + tile] = lax.dot_general(
                tok[...], heads[0][low : low + tile, :], dims, preferred_element_type=F32
            )
        for block in blocks:
            block.wait()
        for low in range(0, rows, tile):
            scores[:, rows + low : rows + low + tile] = lax.dot_general(
                tok[...], held[low : low + tile, :], dims, preferred_element_type=F32
            )
    else:
        for n, block in enumerate(blocks):
            block.wait()
            if n + 2 < len(blocks):
                blocks[n + 2].start()
            low = n * chunk
            scores[:, low : low + chunk] = lax.dot_general(
                tok[...], held[low : low + chunk, :], dims, preferred_element_type=F32
            )
    for copy in others:
        copy.wait()
    side_ref[...] = jnp.dot(tok[...], in_ref[...], preferred_element_type=F32)

    step = 512
    best = scores[:, 0:step]
    for low in range(step, 2 * rows, step):
        best = jnp.maximum(best, scores[:, low : low + step])
    best = jnp.max(best, axis=1, keepdims=True)
    total = None
    mixed = None
    for low in range(0, 2 * rows, step):
        power = jnp.exp(scores[:, low : low + step] - best)
        total = power if low == 0 else total + power
        proj = projs[low // rows][low % rows : low % rows + step, :]
        part = jnp.dot(power.astype(BF), proj, preferred_element_type=F32)
        mixed = part if low == 0 else mixed + part
    total = jnp.sum(total, axis=1, keepdims=True)
    out_ref[...] = mixed / total
    lse_ref[...] = jnp.broadcast_to(best + jnp.log(total), lse_ref.shape)


def flash(pieces, own, sib, proj_own, proj_sib, in_proj, limit=None):
    sizes = tuple(p.shape[0] for p in pieces)
    n = sum(sizes)
    stream = limit is not None
    rows, depth = own.shape
    rank = proj_own.shape[1]
    here = pl.BlockSpec(memory_space=pltpu.VMEM)
    away = pl.BlockSpec(memory_space=pl.ANY)
    extra = []
    if stream:
        extra = [pltpu.VMEM(a.shape, BF) for a in (proj_own, proj_sib, in_proj)]
        extra.append(pltpu.SemaphoreType.DMA((3,)))
    return pl.pallas_call(
        functools.partial(flash_kernel, sizes, stream),
        in_specs=[away] * len(pieces) + ([away] * 5 if stream else [here, away, here, here, here]),
        out_specs=[here] * 3,
        out_shape=[jax.ShapeDtypeStruct((n, rank), F32)] * 3,
        scratch_shapes=[
            pltpu.VMEM((n, depth), BF),
            pltpu.VMEM((2 * rows if stream else rows, depth), BF),
            pltpu.VMEM((n, 2 * rows), F32),
            pltpu.SemaphoreType.DMA((len(pieces),)),
            pltpu.SemaphoreType.DMA((4 if stream else 2,)),
        ]
        + extra,
        compiler_params=pltpu.CompilerParams(vmem_limit_bytes=(limit << 20) if stream else LIMIT),
        cost_estimate=pl.CostEstimate(
            flops=2 * n * 2 * rows * depth, bytes_accessed=n * depth * 2, transcendentals=0
        ),
    )(*pieces, own, sib, proj_own, proj_sib, in_proj)


def hot_kernel(where, targets_ref, own_ref, sib_ref, out_ref):
    local = out_ref.shape[1]
    total = jnp.zeros(out_ref.shape, F32)
    for which, proj_ref in enumerate((own_ref, sib_ref)):
        for first in range(0, proj_ref.shape[0], TILE):
            ids = where[which] + first + lax.broadcasted_iota(jnp.int32, (TILE, local), 0)
            hot = jnp.where(ids == targets_ref[...], 1.0, 0.0).astype(BF)
            total += lax.dot_general(
                proj_ref[first : first + TILE, :],
                hot,
                (((0,), (0,)), ((), ())),
                preferred_element_type=F32,
            )
    out_ref[...] = total


def hot_rows(where, targets, proj_own, proj_sib):
    here = pl.BlockSpec(memory_space=pltpu.VMEM)
    return pl.pallas_call(
        hot_kernel,
        in_specs=[pl.BlockSpec(memory_space=pltpu.SMEM), here, here, here],
        out_specs=here,
        out_shape=jax.ShapeDtypeStruct((proj_own.shape[1], targets.shape[1]), F32),
        compiler_params=pltpu.CompilerParams(vmem_limit_bytes=16 * 1024 * 1024),
        cost_estimate=pl.CostEstimate(
            flops=2 * 128 * 2048 * 1024, bytes_accessed=1 << 20, transcendentals=0
        ),
    )(where, targets, proj_own, proj_sib)


def pack_kernel(place, *refs):
    outs, lses, sides = refs[0:3], refs[3:6], refs[6:9]
    hot_ref, send_ref, side_ref, out_nat, lse_nat = refs[9:]
    k = place[0]
    spot = [place[1], place[2], place[3], place[4]]

    def put(slot, quarter, source, start, rows, into=0):
        for h in range(rows // 32):
            group = quarter * 2 + into + h
            at = slice(start + 32 * h, start + 32 * h + 32)
            out_nat[group, spot[slot]] = outs[source][at, :]
            lse_nat[group, spot[slot]] = lses[source][at, :]
            side_ref[group, spot[slot]] = sides[source][at, :]

    ky, kz, kd = k ^ 2, k ^ 1, k ^ 3
    for q in range(4):
        put(0, q, 0, 64 * q, 64)
    for n, (slot, quarter) in enumerate(
        [(1, k), (2, k), (1, ky), (2, ky), (1, kz), (2, kz), (3, k), (1, kd)]
    ):
        put(slot, quarter, 1, 64 * n, 64)
    put(3, ky, 2, 0, 64)
    put(2, kd, 2, 64, 32)
    put(3, kz, 2, 96, 64)
    put(2, kd, 2, 160, 32, into=1)
    put(3, kd, 2, 192, 64)

    for group in range(8):
        mixed = jnp.transpose(out_nat[group].reshape(128, 128)).reshape(16, 8, 128)
        lse = jnp.transpose(lse_nat[group].reshape(128, 128))[0:8, :]
        high = lse.astype(BF).astype(F32)
        rest = lse - high
        middle = rest.astype(BF).astype(F32)
        low = rest - middle
        line = lax.broadcasted_iota(jnp.int32, (8, 128), 0)
        stats = jnp.where(
            line == 0, high, jnp.where(line == 1, middle, jnp.where(line == 2, low, 0.0))
        )
        hot = hot_ref[:, group * 128 : group * 128 + 128].reshape(16, 8, 128)
        for part in range(16):
            to = (2 * group + part % 2) * 8 + part // 2
            send_ref[to] = jnp.concatenate([mixed[part], hot[part], stats], axis=0).astype(BF)


def pack(place, results, hot):
    outs, lses, sides = zip(*results)
    return pl.pallas_call(
        pack_kernel,
        in_specs=[pl.BlockSpec(memory_space=pltpu.SMEM)]
        + [pl.BlockSpec(memory_space=pltpu.VMEM)] * 10,
        out_specs=[pl.BlockSpec(memory_space=pltpu.VMEM)] * 2,
        out_shape=[
            jax.ShapeDtypeStruct((128, 24, 128), BF),
            jax.ShapeDtypeStruct((8, 4, 32, 128), F32),
        ],
        scratch_shapes=[pltpu.VMEM((8, 4, 32, 128), F32)] * 2,
        compiler_params=pltpu.CompilerParams(vmem_limit_bytes=16 * 1024 * 1024),
    )(place, *outs, *lses, *sides, hot)


def merge_kernel(got_ref, out_ref):
    lse = (
        got_ref[:, 16:24, :].astype(F32)
    )
    lse = lse[:, 0:1, :] + lse[:, 1:2, :] + lse[:, 2:3, :]
    source = lax.broadcasted_iota(jnp.int32, (128, 1, 128), 0)
    lane = lax.broadcasted_iota(jnp.int32, (128, 1, 128), 2)
    x = lax.div(lax.rem(source, 8), 2)
    c = lax.rem(source, 2)
    other = lax.div(lane, 32) == lax.rem(x + 1, 4)
    kind = jnp.where(other, 1 - c, c)
    halves = []
    for which in range(2):
        mine = kind == which
        best = jnp.max(jnp.where(mine, lse, -3.0e38), axis=0, keepdims=True)
        weight = jnp.where(mine, jnp.exp(jnp.minimum(lse - best, 0.0)), 0.0)
        total = jnp.sum(weight, axis=0)
        mixed = jnp.sum(weight * got_ref[:, 0:8, :].astype(F32), axis=0)
        hot = jnp.sum(jnp.where(mine, got_ref[:, 8:16, :].astype(F32), 0.0), axis=0)
        halves.append(mixed / total - hot)
    both = jnp.concatenate(halves, axis=1)
    for copy in range(16):
        out_ref[copy] = both


def merge(got):
    return pl.pallas_call(
        merge_kernel,
        in_specs=[pl.BlockSpec(memory_space=pltpu.VMEM)],
        out_specs=pl.BlockSpec(memory_space=pltpu.VMEM),
        out_shape=jax.ShapeDtypeStruct((16, 8, 256), F32),
        compiler_params=pltpu.CompilerParams(vmem_limit_bytes=16 * 1024 * 1024),
    )(got)


def score_kernel(
    flags, out_ref, own_hbm, sib_hbm, seq_ref, store_ref, result_ref, own_ref, sib_ref, store, sems, side_sem
):
    rows = store.shape[0] // 8
    copies = [
        pltpu.make_async_copy(
            store_ref.at[n * rows : (n + 1) * rows, :],
            store.at[n * rows : (n + 1) * rows, :],
            sems.at[n],
        )
        for n in range(8)
    ]
    sides = [
        pltpu.make_async_copy(own_hbm, own_ref, side_sem.at[0]),
        pltpu.make_async_copy(sib_hbm, sib_ref, side_sem.at[1]),
    ]
    for copy in sides + copies[:3]:
        copy.start()
    for copy in sides:
        copy.wait()
    total = jnp.zeros((256, 128), F32)
    for group in range(8):
        out = jnp.concatenate([out_ref[2 * group], out_ref[2 * group + 1]], axis=0)
        ids = seq_ref[group : group + 1, :]
        member = lax.broadcasted_iota(jnp.int32, (16, 256), 0) == ids
        spread = jnp.where(member[None, :, :], out[:, None, :], 0.0).reshape(256, 256)
        first, second = [], []
        for spot in range(4):
            own, sib = own_ref[group, spot], sib_ref[group, spot]
            keep = flags[spot] == 0
            first.append(jnp.where(keep, own, sib))
            second.append(jnp.where(keep, sib, own))
        side = jnp.concatenate(first + second, axis=0)
        spread_high = spread.astype(BF)
        spread_low = (spread - spread_high.astype(F32)).astype(BF)
        side_high = side.astype(BF)
        side_low = (side - side_high.astype(F32)).astype(BF)
        for a, b in (
            (spread_high, side_high),
            (spread_high, side_low),
            (spread_low, side_high),
        ):
            total += jnp.dot(a, b, preferred_element_type=F32)
    grads = jnp.concatenate(
        [total[i * 16 : (i + 1) * 16, :].astype(BF) for i in range(16)], axis=1
    )
    for n, copy in enumerate(copies):
        copy.wait()
        if n + 3 < 8:
            copies[n + 3].start()
        result_ref[n] = lax.dot_general(
            grads,
            store[n * rows : (n + 1) * rows, :],
            (((1,), (1,)), ((), ())),
            preferred_element_type=F32,
        )


def score(flags, out, own, sib, seq, store):
    here = pl.BlockSpec(memory_space=pltpu.VMEM)
    away = pl.BlockSpec(memory_space=pl.ANY)
    return pl.pallas_call(
        score_kernel,
        in_specs=[
            pl.BlockSpec(memory_space=pltpu.SMEM),
            here,
            away,
            away,
            here,
            away,
        ],
        out_specs=here,
        out_shape=jax.ShapeDtypeStruct((8, SEQS, store.shape[0] // 8), F32),
        scratch_shapes=[
            pltpu.VMEM(own.shape, F32),
            pltpu.VMEM(own.shape, F32),
            pltpu.VMEM(store.shape, BF),
            pltpu.SemaphoreType.DMA((8,)),
            pltpu.SemaphoreType.DMA((2,)),
        ],
        compiler_params=pltpu.CompilerParams(vmem_limit_bytes=48 * 1024 * 1024),
    )(flags, out, own, sib, seq, store)


def by_place(per_token):
    table = per_token.reshape(4, 2, 256)
    return jnp.stack([table[:, 0], jnp.roll(table[:, 1], 2, axis=0)])


def on_device(hidden, out_head, out_proj, in_proj, targets, seq_ids, grad_store):
    y, z, x, c = (lax.axis_index(name) for name in ALL)
    k = 2 * (y % 2) + z % 2
    sign = 1 - 2 * c
    rows = out_head.shape[0]

    mine = lax.dynamic_slice_in_dim(hidden, k * 64, 64, 0)

    near_a = move(mine, along_x)
    near_b = move(mine, along_x_crossed)
    head_sib = move(out_head, to_sibling)
    proj_sib = move(out_proj, to_sibling)
    again, proj_sib = lax.optimization_barrier((hidden, proj_sib))
    mine_d = lax.dynamic_slice_in_dim(again, (3 - k) * 64, 64, 0)

    first_row = lax.axis_index(ALL) * rows
    sib_row = (lax.axis_index(ALL) + sign) * rows
    places = jnp.arange(4, dtype=jnp.int32)
    kinds = jnp.where(places == (x + 1) % 4, 1 - c, c)
    target_table = by_place(targets)
    local_targets = jnp.where(kinds[:, None] == 0, target_table[0], target_table[1])
    local_targets = local_targets.reshape(4, 8, 32).transpose(1, 0, 2).reshape(1, 1024)
    seq_table = by_place(seq_ids).reshape(2, 4, 8, 32).transpose(2, 0, 1, 3).reshape(8, 256)

    hot = hot_rows(jnp.stack([first_row, sib_row]), local_targets, out_proj, proj_sib)

    mine_d, near_a, head_sib, hot = lax.optimization_barrier((mine_d, near_a, head_sib, hot))
    near, ahead = rows_of(
        ((0, 0, 64, 0, 0), (1, 0, 64, 0, 64), (0, 0, 64, 1, 0), (2, 0, 64, 1, 64)),
        [near_a, near_b, mine_d],
        [128, 128],
    )
    near_y = move(near, along_y)
    near_z = move(near, along_z)
    ahead = move(ahead, along_x)
    rest = (out_head, head_sib, out_proj, proj_sib, in_proj)
    first = flash([hidden], *rest, limit=56)
    first, ahead, near_y, near_z = lax.optimization_barrier((first, ahead, near_y, near_z))
    last_y, last_z, far_d = rows_of(
        (
            (0, 0, 64, 0, 0),
            (2, 64, 32, 0, 64),
            (0, 0, 64, 1, 0),
            (1, 96, 32, 1, 64),
            (0, 64, 64, 2, 0),
        ),
        [ahead, near_y, near_z],
        [96, 96, 64],
    )
    last_y = move(last_y, along_y)
    last_z = move(last_z, along_z)
    far_d = move(far_d, along_x)
    second = flash([near, near_y, near_z, ahead], *rest, limit=44)
    third = flash([last_y, last_z, far_d], *rest)
    place = jnp.stack(
        [
            k,
            (x + 2 * c) % 4,
            (x - sign + 2 * c + 4) % 4,
            (x - sign + 2 * (1 - c) + 4) % 4,
            (x + 2 + 2 * c) % 4,
        ]
    ).astype(jnp.int32)
    send, side = pack(place, (first, second, third), hot)
    side_sib = move(side, to_sibling)

    got = lax.all_to_all(send, ALL, 0, 0, tiled=True)

    out = lax.all_to_all(merge(got), ("y", "z"), 0, 0, tiled=True)
    partial = score(kinds.astype(jnp.int32), out, side, side_sib, seq_table, grad_store)
    return jnp.sum(lax.all_to_all(partial, ("x", "c"), 0, 0, tiled=True), axis=0).T


def solution(mesh):
    split = Mesh(mesh.devices.reshape(4, 4, 4, 2), ALL)
    everywhere = P(ALL, None)
    return jax.shard_map(
        on_device,
        mesh=split,
        in_specs=(
            P(("x", "c"), None),
            everywhere,
            everywhere,
            P(),
            P(),
            P(),
            P(("y", "z"), ("x", "c")),
        ),
        out_specs=everywhere,
        check_vma=False,
    )
```

```python
import functools

import jax
import jax.numpy as jnp
from jax import lax
from jax.experimental import pallas as pl
from jax.experimental.pallas import tpu as pltpu
from jax.sharding import Mesh
from jax.sharding import PartitionSpec as P

SEQS = 16
ALL = ("y", "z", "x", "c")
TILE = 256
LIMIT = 26 * 1024 * 1024
AHEAD = 2
BF = jnp.bfloat16
F32 = jnp.float32


def index(y, z, x, c):
    return (((y % 4) * 4 + z % 4) * 4 + x % 4) * 2 + c


def move(value, target):
    pairs = [
        (index(y, z, x, c), index(*target(y, z, x, c)))
        for y in range(4)
        for z in range(4)
        for x in range(4)
        for c in range(2)
    ]
    return lax.ppermute(value, ALL, pairs)


def along_x(y, z, x, c):
    return (y, z, x + 1 - 2 * c, c)


def along_x_crossed(y, z, x, c):
    return (y, z, x - 1 + 2 * c, 1 - c)


def along_y(y, z, x, c):
    return (y + 1 - 2 * c, z, x, c)


def along_z(y, z, x, c):
    return (y, z + 1 - 2 * c, x, c)


def to_sibling(y, z, x, c):
    return (y, z, x, 1 - c)


def rows_kernel(plan, count, *refs):
    sources, results, sems = refs[:count], refs[count:-1], refs[-1]
    copies = [
        pltpu.make_async_copy(
            sources[source].at[start : start + rows, :],
            results[to].at[at : at + rows, :],
            sems.at[n],
        )
        for n, (source, start, rows, to, at) in enumerate(plan)
    ]
    for copy in copies:
        copy.start()
    for copy in copies:
        copy.wait()


def rows_of(plan, sources, lengths):
    away = pl.BlockSpec(memory_space=pl.ANY)
    width = sources[0].shape[1]
    return pl.pallas_call(
        functools.partial(rows_kernel, plan, len(sources)),
        in_specs=[away] * len(sources),
        out_specs=[away] * len(lengths),
        out_shape=[jax.ShapeDtypeStruct((n, width), BF) for n in lengths],
        scratch_shapes=[pltpu.SemaphoreType.DMA((len(plan),))],
        compiler_params=pltpu.CompilerParams(vmem_limit_bytes=16 * 1024 * 1024),
        cost_estimate=pl.CostEstimate(
            flops=0, bytes_accessed=4 * width * sum(lengths), transcendentals=0
        ),
    )(*sources)


def flash_kernel(sizes, stream, *refs):
    count = len(sizes)
    pieces, heads = refs[:count], refs[count : count + 2]
    projs, in_ref = refs[count + 2 : count + 4], refs[count + 4]
    out_ref, lse_ref, side_ref = refs[count + 5 : count + 8]
    tok, held, scores, sems, head_sem = refs[count + 8 : count + 13]
    rows = heads[0].shape[0]

    copies = []
    at = 0
    for number, (size, piece) in enumerate(zip(sizes, pieces)):
        copies.append(pltpu.make_async_copy(piece, tok.at[at : at + size, :], sems.at[number]))
        at += size
    blocks = []
    bounds = (0, 256, 512, 1024, 1536, 2048) if stream else (1024, 1536, 2048)
    for low, high in zip(bounds, bounds[1:]):
        head, shift = heads[low // rows], low // rows * rows
        at = low if stream else low - rows
        blocks.append(
            pltpu.make_async_copy(
                head.at[low - shift : high - shift, :],
                held.at[at : at + high - low, :],
                head_sem.at[len(blocks)],
            )
        )
    others = []
    if stream:
        far = (*projs, in_ref)
        *projs, in_ref = refs[count + 13 : count + 16]
        for n, (source, target) in enumerate(zip(far, (*projs, in_ref))):
            others.append(pltpu.make_async_copy(source, target, refs[count + 16].at[n]))
    for copy in copies + blocks[:AHEAD] + others:
        copy.start()
    for copy in copies:
        copy.wait()

    dims = (((1,), (1,)), ((), ()))
    tile = 1024 if tok.shape[0] <= 256 else 512
    if not stream:
        for low in range(0, rows, tile):
            scores[:, low : low + tile] = lax.dot_general(
                tok[...], heads[0][low : low + tile, :], dims, preferred_element_type=F32
            )
        for block in blocks:
            block.wait()
        for low in range(0, rows, tile):
            scores[:, rows + low : rows + low + tile] = lax.dot_general(
                tok[...], held[low : low + tile, :], dims, preferred_element_type=F32
            )
    else:
        for n, block in enumerate(blocks):
            block.wait()
            if n + AHEAD < len(blocks):
                blocks[n + AHEAD].start()
            low, high = bounds[n], bounds[n + 1]
            scores[:, low:high] = lax.dot_general(
                tok[...], held[low:high, :], dims, preferred_element_type=F32
            )
    for copy in others:
        copy.wait()
    side_ref[...] = jnp.dot(tok[...], in_ref[...], preferred_element_type=F32)

    step = 512
    best = scores[:, 0:step]
    for low in range(step, 2 * rows, step):
        best = jnp.maximum(best, scores[:, low : low + step])
    best = jnp.max(best, axis=1, keepdims=True)
    total = None
    mixed = None
    for low in range(0, 2 * rows, step):
        power = jnp.exp(scores[:, low : low + step] - best)
        total = power if low == 0 else total + power
        proj = projs[low // rows][low % rows : low % rows + step, :]
        part = jnp.dot(power.astype(BF), proj, preferred_element_type=F32)
        mixed = part if low == 0 else mixed + part
    total = jnp.sum(total, axis=1, keepdims=True)
    out_ref[...] = mixed / total
    lse_ref[...] = jnp.broadcast_to(best + jnp.log(total), lse_ref.shape)


def flash(pieces, own, sib, proj_own, proj_sib, in_proj, limit=None):
    sizes = tuple(p.shape[0] for p in pieces)
    n = sum(sizes)
    stream = limit is not None
    rows, depth = own.shape
    rank = proj_own.shape[1]
    here = pl.BlockSpec(memory_space=pltpu.VMEM)
    away = pl.BlockSpec(memory_space=pl.ANY)
    extra = []
    if stream:
        extra = [pltpu.VMEM(a.shape, BF) for a in (proj_own, proj_sib, in_proj)]
        extra.append(pltpu.SemaphoreType.DMA((3,)))
    return pl.pallas_call(
        functools.partial(flash_kernel, sizes, stream),
        in_specs=[away] * len(pieces) + ([away] * 5 if stream else [here, away, here, here, here]),
        out_specs=[here] * 3,
        out_shape=[jax.ShapeDtypeStruct((n, rank), F32)] * 3,
        scratch_shapes=[
            pltpu.VMEM((n, depth), BF),
            pltpu.VMEM((2 * rows if stream else rows, depth), BF),
            pltpu.VMEM((n, 2 * rows), F32),
            pltpu.SemaphoreType.DMA((len(pieces),)),
            pltpu.SemaphoreType.DMA((5 if stream else 2,)),
        ]
        + extra,
        compiler_params=pltpu.CompilerParams(vmem_limit_bytes=(limit << 20) if stream else LIMIT),
        cost_estimate=pl.CostEstimate(
            flops=2 * n * 2 * rows * depth, bytes_accessed=n * depth * 2, transcendentals=0
        ),
    )(*pieces, own, sib, proj_own, proj_sib, in_proj)


def hot_kernel(where, targets_ref, own_ref, sib_ref, out_ref):
    local = out_ref.shape[1]
    total = jnp.zeros(out_ref.shape, F32)
    for which, proj_ref in enumerate((own_ref, sib_ref)):
        for first in range(0, proj_ref.shape[0], TILE):
            ids = where[which] + first + lax.broadcasted_iota(jnp.int32, (TILE, local), 0)
            hot = jnp.where(ids == targets_ref[...], 1.0, 0.0).astype(BF)
            total += lax.dot_general(
                proj_ref[first : first + TILE, :],
                hot,
                (((0,), (0,)), ((), ())),
                preferred_element_type=F32,
            )
    out_ref[...] = total


def hot_rows(where, targets, proj_own, proj_sib):
    here = pl.BlockSpec(memory_space=pltpu.VMEM)
    return pl.pallas_call(
        hot_kernel,
        in_specs=[pl.BlockSpec(memory_space=pltpu.SMEM), here, here, here],
        out_specs=here,
        out_shape=jax.ShapeDtypeStruct((proj_own.shape[1], targets.shape[1]), F32),
        compiler_params=pltpu.CompilerParams(vmem_limit_bytes=16 * 1024 * 1024),
        cost_estimate=pl.CostEstimate(
            flops=2 * 128 * 2048 * 1024, bytes_accessed=1 << 20, transcendentals=0
        ),
    )(where, targets, proj_own, proj_sib)


def pack_kernel(place, *refs):
    outs, lses, sides = refs[0:3], refs[3:6], refs[6:9]
    hot_ref, send_ref, side_ref, out_nat, lse_nat = refs[9:]
    k = place[0]
    spot = [place[1], place[2], place[3], place[4]]

    def put(slot, quarter, source, start, rows, into=0):
        for h in range(rows // 32):
            group = quarter * 2 + into + h
            at = slice(start + 32 * h, start + 32 * h + 32)
            out_nat[group, spot[slot]] = outs[source][at, :]
            lse_nat[group, spot[slot]] = lses[source][at, :]
            side_ref[group, spot[slot]] = sides[source][at, :]

    ky, kz, kd = k ^ 2, k ^ 1, k ^ 3
    for q in range(4):
        put(0, q, 0, 64 * q, 64)
    for n, (slot, quarter) in enumerate(
        [(1, k), (2, k), (1, ky), (2, ky), (1, kz), (2, kz), (3, k), (1, kd)]
    ):
        put(slot, quarter, 1, 64 * n, 64)
    put(3, ky, 2, 0, 64)
    put(2, kd, 2, 64, 32)
    put(3, kz, 2, 96, 64)
    put(2, kd, 2, 160, 32, into=1)
    put(3, kd, 2, 192, 64)

    for group in range(8):
        mixed = jnp.transpose(out_nat[group].reshape(128, 128)).reshape(16, 8, 128)
        lse = jnp.transpose(lse_nat[group].reshape(128, 128))[0:8, :]
        high = lse.astype(BF).astype(F32)
        rest = lse - high
        middle = rest.astype(BF).astype(F32)
        low = rest - middle
        line = lax.broadcasted_iota(jnp.int32, (8, 128), 0)
        stats = jnp.where(
            line == 0, high, jnp.where(line == 1, middle, jnp.where(line == 2, low, 0.0))
        )
        hot = hot_ref[:, group * 128 : group * 128 + 128].reshape(16, 8, 128)
        for part in range(16):
            to = (2 * group + part % 2) * 8 + part // 2
            send_ref[to] = jnp.concatenate([mixed[part], hot[part], stats], axis=0).astype(BF)


def pack(place, results, hot):
    outs, lses, sides = zip(*results)
    return pl.pallas_call(
        pack_kernel,
        in_specs=[pl.BlockSpec(memory_space=pltpu.SMEM)]
        + [pl.BlockSpec(memory_space=pltpu.VMEM)] * 10,
        out_specs=[pl.BlockSpec(memory_space=pltpu.VMEM)] * 2,
        out_shape=[
            jax.ShapeDtypeStruct((128, 24, 128), BF),
            jax.ShapeDtypeStruct((8, 4, 32, 128), F32),
        ],
        scratch_shapes=[pltpu.VMEM((8, 4, 32, 128), F32)] * 2,
        compiler_params=pltpu.CompilerParams(vmem_limit_bytes=16 * 1024 * 1024),
    )(place, *outs, *lses, *sides, hot)


def merge_kernel(got_ref, out_ref):
    lse = (
        got_ref[:, 16:24, :].astype(F32)
    )
    lse = lse[:, 0:1, :] + lse[:, 1:2, :] + lse[:, 2:3, :]
    source = lax.broadcasted_iota(jnp.int32, (128, 1, 128), 0)
    lane = lax.broadcasted_iota(jnp.int32, (128, 1, 128), 2)
    x = lax.div(lax.rem(source, 8), 2)
    c = lax.rem(source, 2)
    other = lax.div(lane, 32) == lax.rem(x + 1, 4)
    kind = jnp.where(other, 1 - c, c)
    halves = []
    for which in range(2):
        mine = kind == which
        best = jnp.max(jnp.where(mine, lse, -3.0e38), axis=0, keepdims=True)
        weight = jnp.where(mine, jnp.exp(jnp.minimum(lse - best, 0.0)), 0.0)
        total = jnp.sum(weight, axis=0)
        mixed = jnp.sum(weight * got_ref[:, 0:8, :].astype(F32), axis=0)
        hot = jnp.sum(jnp.where(mine, got_ref[:, 8:16, :].astype(F32), 0.0), axis=0)
        halves.append(mixed / total - hot)
    both = jnp.concatenate(halves, axis=1)
    for copy in range(16):
        out_ref[copy] = both


def merge(got):
    return pl.pallas_call(
        merge_kernel,
        in_specs=[pl.BlockSpec(memory_space=pltpu.VMEM)],
        out_specs=pl.BlockSpec(memory_space=pltpu.VMEM),
        out_shape=jax.ShapeDtypeStruct((16, 8, 256), F32),
        compiler_params=pltpu.CompilerParams(vmem_limit_bytes=16 * 1024 * 1024),
    )(got)


def score_kernel(
    flags, out_ref, own_hbm, sib_hbm, seq_ref, store_ref, result_ref, own_ref, sib_ref, store, sems, side_sem
):
    rows = store.shape[0] // 8
    copies = [
        pltpu.make_async_copy(
            store_ref.at[n * rows : (n + 1) * rows, :],
            store.at[n * rows : (n + 1) * rows, :],
            sems.at[n],
        )
        for n in range(8)
    ]
    sides = [
        pltpu.make_async_copy(own_hbm, own_ref, side_sem.at[0]),
        pltpu.make_async_copy(sib_hbm, sib_ref, side_sem.at[1]),
    ]
    for copy in sides + copies[:3]:
        copy.start()
    for copy in sides:
        copy.wait()
    total = jnp.zeros((256, 128), F32)
    for group in range(8):
        out = jnp.concatenate([out_ref[2 * group], out_ref[2 * group + 1]], axis=0)
        ids = seq_ref[group : group + 1, :]
        member = lax.broadcasted_iota(jnp.int32, (16, 256), 0) == ids
        spread = jnp.where(member[None, :, :], out[:, None, :], 0.0).reshape(256, 256)
        first, second = [], []
        for spot in range(4):
            own, sib = own_ref[group, spot], sib_ref[group, spot]
            keep = flags[spot] == 0
            first.append(jnp.where(keep, own, sib))
            second.append(jnp.where(keep, sib, own))
        side = jnp.concatenate(first + second, axis=0)
        spread_high = spread.astype(BF)
        spread_low = (spread - spread_high.astype(F32)).astype(BF)
        side_high = side.astype(BF)
        side_low = (side - side_high.astype(F32)).astype(BF)
        for a, b in (
            (spread_high, side_high),
            (spread_high, side_low),
            (spread_low, side_high),
        ):
            total += jnp.dot(a, b, preferred_element_type=F32)
    grads = jnp.concatenate(
        [total[i * 16 : (i + 1) * 16, :].astype(BF) for i in range(16)], axis=1
    )
    for n, copy in enumerate(copies):
        copy.wait()
        if n + 3 < 8:
            copies[n + 3].start()
        result_ref[n] = lax.dot_general(
            grads,
            store[n * rows : (n + 1) * rows, :],
            (((1,), (1,)), ((), ())),
            preferred_element_type=F32,
        )


def score(flags, out, own, sib, seq, store):
    here = pl.BlockSpec(memory_space=pltpu.VMEM)
    away = pl.BlockSpec(memory_space=pl.ANY)
    return pl.pallas_call(
        score_kernel,
        in_specs=[
            pl.BlockSpec(memory_space=pltpu.SMEM),
            here,
            away,
            away,
            here,
            away,
        ],
        out_specs=here,
        out_shape=jax.ShapeDtypeStruct((8, SEQS, store.shape[0] // 8), F32),
        scratch_shapes=[
            pltpu.VMEM(own.shape, F32),
            pltpu.VMEM(own.shape, F32),
            pltpu.VMEM(store.shape, BF),
            pltpu.SemaphoreType.DMA((8,)),
            pltpu.SemaphoreType.DMA((2,)),
        ],
        compiler_params=pltpu.CompilerParams(vmem_limit_bytes=48 * 1024 * 1024),
    )(flags, out, own, sib, seq, store)


def by_place(per_token):
    table = per_token.reshape(4, 2, 256)
    return jnp.stack([table[:, 0], jnp.roll(table[:, 1], 2, axis=0)])


def on_device(hidden, out_head, out_proj, in_proj, targets, seq_ids, grad_store):
    y, z, x, c = (lax.axis_index(name) for name in ALL)
    k = 2 * (y % 2) + z % 2
    sign = 1 - 2 * c
    rows = out_head.shape[0]

    mine = lax.dynamic_slice_in_dim(hidden, k * 64, 64, 0)

    near_a = move(mine, along_x)
    near_b = move(mine, along_x_crossed)
    head_sib = move(out_head, to_sibling)
    proj_sib = move(out_proj, to_sibling)

    first_row = lax.axis_index(ALL) * rows
    sib_row = (lax.axis_index(ALL) + sign) * rows
    places = jnp.arange(4, dtype=jnp.int32)
    kinds = jnp.where(places == (x + 1) % 4, 1 - c, c)
    target_table = by_place(targets)
    local_targets = jnp.where(kinds[:, None] == 0, target_table[0], target_table[1])
    local_targets = local_targets.reshape(4, 8, 32).transpose(1, 0, 2).reshape(1, 1024)
    seq_table = by_place(seq_ids).reshape(2, 4, 8, 32).transpose(2, 0, 1, 3).reshape(8, 256)

    again, local_targets = lax.optimization_barrier((hidden, local_targets))
    mine_d = lax.dynamic_slice_in_dim(again, (3 - k) * 64, 64, 0)

    mine_d, near_a = lax.optimization_barrier((mine_d, near_a))
    near, ahead = rows_of(
        ((0, 0, 64, 0, 0), (1, 0, 64, 0, 64), (0, 0, 64, 1, 0), (2, 0, 64, 1, 64)),
        [near_a, near_b, mine_d],
        [128, 128],
    )
    near_y = move(near, along_y)
    near_z = move(near, along_z)
    ahead = move(ahead, along_x)
    rest = (out_head, head_sib, out_proj, proj_sib, in_proj)
    first = flash([hidden], *rest)
    first, ahead, near_y, near_z = lax.optimization_barrier((first, ahead, near_y, near_z))
    first, local_targets = lax.optimization_barrier((first, local_targets))
    hot = hot_rows(jnp.stack([first_row, sib_row]), local_targets, out_proj, proj_sib)
    last_y, last_z, far_d = rows_of(
        (
            (0, 0, 64, 0, 0),
            (2, 64, 32, 0, 64),
            (0, 0, 64, 1, 0),
            (1, 96, 32, 1, 64),
            (0, 64, 64, 2, 0),
        ),
        [ahead, near_y, near_z],
        [96, 96, 64],
    )
    last_y = move(last_y, along_y)
    last_z = move(last_z, along_z)
    far_d = move(far_d, along_x)
    second = flash([near, near_y, near_z, ahead], *rest)
    third = flash([last_y, last_z, far_d], *rest)
    place = jnp.stack(
        [
            k,
            (x + 2 * c) % 4,
            (x - sign + 2 * c + 4) % 4,
            (x - sign + 2 * (1 - c) + 4) % 4,
            (x + 2 + 2 * c) % 4,
        ]
    ).astype(jnp.int32)
    send, side = pack(place, (first, second, third), hot)
    side_sib = move(side, to_sibling)

    got = lax.all_to_all(send, ALL, 0, 0, tiled=True)

    out = lax.all_to_all(merge(got), ("y", "z"), 0, 0, tiled=True)
    partial = score(kinds.astype(jnp.int32), out, side, side_sib, seq_table, grad_store)
    return jnp.sum(lax.all_to_all(partial, ("x", "c"), 0, 0, tiled=True), axis=0).T


def solution(mesh):
    split = Mesh(mesh.devices.reshape(4, 4, 4, 2), ALL)
    everywhere = P(ALL, None)
    return jax.shard_map(
        on_device,
        mesh=split,
        in_specs=(
            P(("x", "c"), None),
            everywhere,
            everywhere,
            P(),
            P(),
            P(),
            P(("y", "z"), ("x", "c")),
        ),
        out_specs=everywhere,
        check_vma=False,
    )
```

```python
import functools

import jax
import jax.numpy as jnp
from jax import lax
from jax.experimental import pallas as pl
from jax.experimental.pallas import tpu as pltpu
from jax.sharding import Mesh
from jax.sharding import PartitionSpec as P

SEQS = 16
ALL = ("y", "z", "x", "c")
TILE = 256
LIMIT = 26 * 1024 * 1024
AHEAD = 2
BF = jnp.bfloat16
F32 = jnp.float32


def index(y, z, x, c):
    return (((y % 4) * 4 + z % 4) * 4 + x % 4) * 2 + c


def move(value, target):
    pairs = [
        (index(y, z, x, c), index(*target(y, z, x, c)))
        for y in range(4)
        for z in range(4)
        for x in range(4)
        for c in range(2)
    ]
    return lax.ppermute(value, ALL, pairs)


def along_x(y, z, x, c):
    return (y, z, x + 1 - 2 * c, c)


def along_x_crossed(y, z, x, c):
    return (y, z, x - 1 + 2 * c, 1 - c)


def along_y(y, z, x, c):
    return (y + 1 - 2 * c, z, x, c)


def along_z(y, z, x, c):
    return (y, z + 1 - 2 * c, x, c)


def to_sibling(y, z, x, c):
    return (y, z, x, 1 - c)


def rows_kernel(plan, count, *refs):
    sources, results, sems = refs[:count], refs[count:-1], refs[-1]
    copies = [
        pltpu.make_async_copy(
            sources[source].at[start : start + rows, :],
            results[to].at[at : at + rows, :],
            sems.at[n],
        )
        for n, (source, start, rows, to, at) in enumerate(plan)
    ]
    for copy in copies:
        copy.start()
    for copy in copies:
        copy.wait()


def rows_of(plan, sources, lengths):
    away = pl.BlockSpec(memory_space=pl.ANY)
    width = sources[0].shape[1]
    return pl.pallas_call(
        functools.partial(rows_kernel, plan, len(sources)),
        in_specs=[away] * len(sources),
        out_specs=[away] * len(lengths),
        out_shape=[jax.ShapeDtypeStruct((n, width), BF) for n in lengths],
        scratch_shapes=[pltpu.SemaphoreType.DMA((len(plan),))],
        compiler_params=pltpu.CompilerParams(vmem_limit_bytes=16 * 1024 * 1024),
        cost_estimate=pl.CostEstimate(
            flops=0, bytes_accessed=4 * width * sum(lengths), transcendentals=0
        ),
    )(*sources)


def flash_kernel(sizes, stream, *refs):
    count = len(sizes)
    pieces, heads = refs[:count], refs[count : count + 2]
    projs, in_ref = refs[count + 2 : count + 4], refs[count + 4]
    out_ref, lse_ref, side_ref = refs[count + 5 : count + 8]
    tok, held, scores, sems, head_sem = refs[count + 8 : count + 13]
    rows = heads[0].shape[0]

    copies = []
    at = 0
    for number, (size, piece) in enumerate(zip(sizes, pieces)):
        copies.append(pltpu.make_async_copy(piece, tok.at[at : at + size, :], sems.at[number]))
        at += size
    blocks = []
    bounds = (0, 256, 512, 1024, 1536, 2048) if stream else (1024, 1536, 2048)
    for low, high in zip(bounds, bounds[1:]):
        head, shift = heads[low // rows], low // rows * rows
        at = low if stream else low - rows
        blocks.append(
            pltpu.make_async_copy(
                head.at[low - shift : high - shift, :],
                held.at[at : at + high - low, :],
                head_sem.at[len(blocks)],
            )
        )
    others = []
    if stream:
        far = (*projs, in_ref)
        *projs, in_ref = refs[count + 13 : count + 16]
        for n, (source, target) in enumerate(zip(far, (*projs, in_ref))):
            others.append(pltpu.make_async_copy(source, target, refs[count + 16].at[n]))
    for copy in copies + blocks[:AHEAD] + others:
        copy.start()
    for copy in copies:
        copy.wait()

    dims = (((1,), (1,)), ((), ()))
    tile = 1024 if tok.shape[0] <= 256 else 512
    if not stream:
        for low in range(0, rows, tile):
            scores[:, low : low + tile] = lax.dot_general(
                tok[...], heads[0][low : low + tile, :], dims, preferred_element_type=F32
            )
        for block in blocks:
            block.wait()
        for low in range(0, rows, tile):
            scores[:, rows + low : rows + low + tile] = lax.dot_general(
                tok[...], held[low : low + tile, :], dims, preferred_element_type=F32
            )
    else:
        for n, block in enumerate(blocks):
            block.wait()
            if n + AHEAD < len(blocks):
                blocks[n + AHEAD].start()
            low, high = bounds[n], bounds[n + 1]
            scores[:, low:high] = lax.dot_general(
                tok[...], held[low:high, :], dims, preferred_element_type=F32
            )
    for copy in others:
        copy.wait()
    side_ref[...] = jnp.dot(tok[...], in_ref[...], preferred_element_type=F32)

    step = 512
    best = scores[:, 0:step]
    for low in range(step, 2 * rows, step):
        best = jnp.maximum(best, scores[:, low : low + step])
    best = jnp.max(best, axis=1, keepdims=True)
    total = None
    mixed = None
    for low in range(0, 2 * rows, step):
        power = jnp.exp(scores[:, low : low + step] - best)
        total = power if low == 0 else total + power
        proj = projs[low // rows][low % rows : low % rows + step, :]
        part = jnp.dot(power.astype(BF), proj, preferred_element_type=F32)
        mixed = part if low == 0 else mixed + part
    total = jnp.sum(total, axis=1, keepdims=True)
    out_ref[...] = mixed / total
    lse_ref[...] = jnp.broadcast_to(best + jnp.log(total), lse_ref.shape)


def flash(pieces, own, sib, proj_own, proj_sib, in_proj, limit=None):
    sizes = tuple(p.shape[0] for p in pieces)
    n = sum(sizes)
    stream = limit is not None
    rows, depth = own.shape
    rank = proj_own.shape[1]
    here = pl.BlockSpec(memory_space=pltpu.VMEM)
    away = pl.BlockSpec(memory_space=pl.ANY)
    extra = []
    if stream:
        extra = [pltpu.VMEM(a.shape, BF) for a in (proj_own, proj_sib, in_proj)]
        extra.append(pltpu.SemaphoreType.DMA((3,)))
    return pl.pallas_call(
        functools.partial(flash_kernel, sizes, stream),
        in_specs=[away] * len(pieces) + ([away] * 5 if stream else [here, away, here, here, here]),
        out_specs=[here] * 3,
        out_shape=[jax.ShapeDtypeStruct((n, rank), F32)] * 3,
        scratch_shapes=[
            pltpu.VMEM((n, depth), BF),
            pltpu.VMEM((2 * rows if stream else rows, depth), BF),
            pltpu.VMEM((n, 2 * rows), F32),
            pltpu.SemaphoreType.DMA((len(pieces),)),
            pltpu.SemaphoreType.DMA((5 if stream else 2,)),
        ]
        + extra,
        compiler_params=pltpu.CompilerParams(vmem_limit_bytes=(limit << 20) if stream else LIMIT),
        cost_estimate=pl.CostEstimate(
            flops=2 * n * 2 * rows * depth, bytes_accessed=n * depth * 2, transcendentals=0
        ),
    )(*pieces, own, sib, proj_own, proj_sib, in_proj)


def hot_kernel(where, targets_ref, own_ref, sib_ref, out_ref):
    local = out_ref.shape[1]
    total = jnp.zeros(out_ref.shape, F32)
    for which, proj_ref in enumerate((own_ref, sib_ref)):
        for first in range(0, proj_ref.shape[0], TILE):
            ids = where[which] + first + lax.broadcasted_iota(jnp.int32, (TILE, local), 0)
            hot = jnp.where(ids == targets_ref[...], 1.0, 0.0).astype(BF)
            total += lax.dot_general(
                proj_ref[first : first + TILE, :],
                hot,
                (((0,), (0,)), ((), ())),
                preferred_element_type=F32,
            )
    out_ref[...] = total


def hot_rows(where, targets, proj_own, proj_sib):
    here = pl.BlockSpec(memory_space=pltpu.VMEM)
    return pl.pallas_call(
        hot_kernel,
        in_specs=[pl.BlockSpec(memory_space=pltpu.SMEM), here, here, here],
        out_specs=here,
        out_shape=jax.ShapeDtypeStruct((proj_own.shape[1], targets.shape[1]), F32),
        compiler_params=pltpu.CompilerParams(vmem_limit_bytes=16 * 1024 * 1024),
        cost_estimate=pl.CostEstimate(
            flops=2 * 128 * 2048 * 1024, bytes_accessed=1 << 20, transcendentals=0
        ),
    )(where, targets, proj_own, proj_sib)


def pack_kernel(place, *refs):
    outs, lses, sides = refs[0:3], refs[3:6], refs[6:9]
    hot_ref, send_ref, side_ref, out_nat, lse_nat = refs[9:]
    k = place[0]
    spot = [place[1], place[2], place[3], place[4]]

    def put(slot, quarter, source, start, rows, into=0):
        for h in range(rows // 32):
            group = quarter * 2 + into + h
            at = slice(start + 32 * h, start + 32 * h + 32)
            out_nat[group, spot[slot]] = outs[source][at, :]
            lse_nat[group, spot[slot]] = lses[source][at, :]
            side_ref[group, spot[slot]] = sides[source][at, :]

    ky, kz, kd = k ^ 2, k ^ 1, k ^ 3
    for q in range(4):
        put(0, q, 0, 64 * q, 64)
    for n, (slot, quarter) in enumerate(
        [(1, k), (2, k), (1, ky), (2, ky), (1, kz), (2, kz), (3, k), (1, kd)]
    ):
        put(slot, quarter, 1, 64 * n, 64)
    put(3, ky, 2, 0, 64)
    put(2, kd, 2, 64, 32)
    put(3, kz, 2, 96, 64)
    put(2, kd, 2, 160, 32, into=1)
    put(3, kd, 2, 192, 64)

    for group in range(8):
        mixed = jnp.transpose(out_nat[group].reshape(128, 128)).reshape(16, 8, 128)
        lse = jnp.transpose(lse_nat[group].reshape(128, 128))[0:8, :]
        high = lse.astype(BF).astype(F32)
        rest = lse - high
        middle = rest.astype(BF).astype(F32)
        low = rest - middle
        line = lax.broadcasted_iota(jnp.int32, (8, 128), 0)
        stats = jnp.where(
            line == 0, high, jnp.where(line == 1, middle, jnp.where(line == 2, low, 0.0))
        )
        hot = hot_ref[:, group * 128 : group * 128 + 128].reshape(16, 8, 128)
        for part in range(16):
            to = (2 * group + part % 2) * 8 + part // 2
            send_ref[to] = jnp.concatenate([mixed[part], hot[part], stats], axis=0).astype(BF)


def pack(place, results, hot):
    outs, lses, sides = zip(*results)
    return pl.pallas_call(
        pack_kernel,
        in_specs=[pl.BlockSpec(memory_space=pltpu.SMEM)]
        + [pl.BlockSpec(memory_space=pltpu.VMEM)] * 10,
        out_specs=[pl.BlockSpec(memory_space=pltpu.VMEM)] * 2,
        out_shape=[
            jax.ShapeDtypeStruct((128, 24, 128), BF),
            jax.ShapeDtypeStruct((8, 4, 32, 128), F32),
        ],
        scratch_shapes=[pltpu.VMEM((8, 4, 32, 128), F32)] * 2,
        compiler_params=pltpu.CompilerParams(vmem_limit_bytes=16 * 1024 * 1024),
    )(place, *outs, *lses, *sides, hot)


def merge_kernel(got_ref, out_ref):
    lse = (
        got_ref[:, 16:24, :].astype(F32)
    )
    lse = lse[:, 0:1, :] + lse[:, 1:2, :] + lse[:, 2:3, :]
    source = lax.broadcasted_iota(jnp.int32, (128, 1, 128), 0)
    lane = lax.broadcasted_iota(jnp.int32, (128, 1, 128), 2)
    x = lax.div(lax.rem(source, 8), 2)
    c = lax.rem(source, 2)
    other = lax.div(lane, 32) == lax.rem(x + 1, 4)
    kind = jnp.where(other, 1 - c, c)
    halves = []
    for which in range(2):
        mine = kind == which
        best = jnp.max(jnp.where(mine, lse, -3.0e38), axis=0, keepdims=True)
        weight = jnp.where(mine, jnp.exp(jnp.minimum(lse - best, 0.0)), 0.0)
        total = jnp.sum(weight, axis=0)
        mixed = jnp.sum(weight * got_ref[:, 0:8, :].astype(F32), axis=0)
        hot = jnp.sum(jnp.where(mine, got_ref[:, 8:16, :].astype(F32), 0.0), axis=0)
        halves.append(mixed / total - hot)
    both = jnp.concatenate(halves, axis=1)
    for copy in range(16):
        out_ref[copy] = both


def merge(got):
    return pl.pallas_call(
        merge_kernel,
        in_specs=[pl.BlockSpec(memory_space=pltpu.VMEM)],
        out_specs=pl.BlockSpec(memory_space=pltpu.VMEM),
        out_shape=jax.ShapeDtypeStruct((16, 8, 256), F32),
        compiler_params=pltpu.CompilerParams(vmem_limit_bytes=16 * 1024 * 1024),
    )(got)


def score_kernel(
    flags, out_ref, own_hbm, sib_hbm, seq_ref, store_ref, result_ref, own_ref, sib_ref, store, sems, side_sem
):
    rows = store.shape[0] // 8
    copies = [
        pltpu.make_async_copy(
            store_ref.at[n * rows : (n + 1) * rows, :],
            store.at[n * rows : (n + 1) * rows, :],
            sems.at[n],
        )
        for n in range(8)
    ]
    sides = [
        pltpu.make_async_copy(own_hbm, own_ref, side_sem.at[0]),
        pltpu.make_async_copy(sib_hbm, sib_ref, side_sem.at[1]),
    ]
    for copy in sides + copies[:3]:
        copy.start()
    for copy in sides:
        copy.wait()
    total = jnp.zeros((256, 128), F32)
    for group in range(8):
        out = jnp.concatenate([out_ref[2 * group], out_ref[2 * group + 1]], axis=0)
        ids = seq_ref[group : group + 1, :]
        member = lax.broadcasted_iota(jnp.int32, (16, 256), 0) == ids
        spread = jnp.where(member[None, :, :], out[:, None, :], 0.0).reshape(256, 256)
        first, second = [], []
        for spot in range(4):
            own, sib = own_ref[group, spot], sib_ref[group, spot]
            keep = flags[spot] == 0
            first.append(jnp.where(keep, own, sib))
            second.append(jnp.where(keep, sib, own))
        side = jnp.concatenate(first + second, axis=0)
        spread_high = spread.astype(BF)
        spread_low = (spread - spread_high.astype(F32)).astype(BF)
        side_high = side.astype(BF)
        side_low = (side - side_high.astype(F32)).astype(BF)
        for a, b in (
            (spread_high, side_high),
            (spread_high, side_low),
            (spread_low, side_high),
        ):
            total += jnp.dot(a, b, preferred_element_type=F32)
    grads = jnp.concatenate(
        [total[i * 16 : (i + 1) * 16, :].astype(BF) for i in range(16)], axis=1
    )
    for n, copy in enumerate(copies):
        copy.wait()
        if n + 3 < 8:
            copies[n + 3].start()
        result_ref[n] = lax.dot_general(
            grads,
            store[n * rows : (n + 1) * rows, :],
            (((1,), (1,)), ((), ())),
            preferred_element_type=F32,
        )


def score(flags, out, own, sib, seq, store):
    here = pl.BlockSpec(memory_space=pltpu.VMEM)
    away = pl.BlockSpec(memory_space=pl.ANY)
    return pl.pallas_call(
        score_kernel,
        in_specs=[
            pl.BlockSpec(memory_space=pltpu.SMEM),
            here,
            away,
            away,
            here,
            away,
        ],
        out_specs=here,
        out_shape=jax.ShapeDtypeStruct((8, SEQS, store.shape[0] // 8), F32),
        scratch_shapes=[
            pltpu.VMEM(own.shape, F32),
            pltpu.VMEM(own.shape, F32),
            pltpu.VMEM(store.shape, BF),
            pltpu.SemaphoreType.DMA((8,)),
            pltpu.SemaphoreType.DMA((2,)),
        ],
        compiler_params=pltpu.CompilerParams(vmem_limit_bytes=48 * 1024 * 1024),
    )(flags, out, own, sib, seq, store)


def by_place(per_token):
    table = per_token.reshape(4, 2, 256)
    return jnp.stack([table[:, 0], jnp.roll(table[:, 1], 2, axis=0)])


def on_device(hidden, out_head, out_proj, in_proj, targets, seq_ids, grad_store):
    y, z, x, c = (lax.axis_index(name) for name in ALL)
    k = 2 * (y % 2) + z % 2
    sign = 1 - 2 * c
    rows = out_head.shape[0]

    mine = lax.dynamic_slice_in_dim(hidden, k * 64, 64, 0)

    near_a = move(mine, along_x)
    near_b = move(mine, along_x_crossed)
    head_sib = move(out_head, to_sibling)
    proj_sib = move(out_proj, to_sibling)

    first_row = lax.axis_index(ALL) * rows
    sib_row = (lax.axis_index(ALL) + sign) * rows
    places = jnp.arange(4, dtype=jnp.int32)
    kinds = jnp.where(places == (x + 1) % 4, 1 - c, c)
    target_table = by_place(targets)
    local_targets = jnp.where(kinds[:, None] == 0, target_table[0], target_table[1])
    local_targets = local_targets.reshape(4, 8, 32).transpose(1, 0, 2).reshape(1, 1024)
    seq_table = by_place(seq_ids).reshape(2, 4, 8, 32).transpose(2, 0, 1, 3).reshape(8, 256)

    again, local_targets = lax.optimization_barrier((hidden, local_targets))
    mine_d = lax.dynamic_slice_in_dim(again, (3 - k) * 64, 64, 0)

    mine_d, near_a, proj_sib = lax.optimization_barrier((mine_d, near_a, proj_sib))
    near, ahead = rows_of(
        ((0, 0, 64, 0, 0), (1, 0, 64, 0, 64), (0, 0, 64, 1, 0), (2, 0, 64, 1, 64)),
        [near_a, near_b, mine_d],
        [128, 128],
    )
    near_y = move(near, along_y)
    near_z = move(near, along_z)
    ahead = move(ahead, along_x)
    rest = (out_head, head_sib, out_proj, proj_sib, in_proj)
    first = flash([hidden], *rest)
    first, ahead, near_y, near_z = lax.optimization_barrier((first, ahead, near_y, near_z))
    first, local_targets = lax.optimization_barrier((first, local_targets))
    hot = hot_rows(jnp.stack([first_row, sib_row]), local_targets, out_proj, proj_sib)
    last_y, last_z, far_d = rows_of(
        (
            (0, 0, 64, 0, 0),
            (2, 64, 32, 0, 64),
            (0, 0, 64, 1, 0),
            (1, 96, 32, 1, 64),
            (0, 64, 64, 2, 0),
        ),
        [ahead, near_y, near_z],
        [96, 96, 64],
    )
    last_y = move(last_y, along_y)
    last_z = move(last_z, along_z)
    far_d = move(far_d, along_x)
    second = flash([near, near_y, near_z, ahead], *rest)
    third = flash([last_y, last_z, far_d], *rest)
    place = jnp.stack(
        [
            k,
            (x + 2 * c) % 4,
            (x - sign + 2 * c + 4) % 4,
            (x - sign + 2 * (1 - c) + 4) % 4,
            (x + 2 + 2 * c) % 4,
        ]
    ).astype(jnp.int32)
    send, side = pack(place, (first, second, third), hot)
    side_sib = move(side, to_sibling)

    got = lax.all_to_all(send, ALL, 0, 0, tiled=True)

    out = lax.all_to_all(merge(got), ("y", "z"), 0, 0, tiled=True)
    partial = score(kinds.astype(jnp.int32), out, side, side_sib, seq_table, grad_store)
    return jnp.sum(lax.all_to_all(partial, ("x", "c"), 0, 0, tiled=True), axis=0).T


def solution(mesh):
    split = Mesh(mesh.devices.reshape(4, 4, 4, 2), ALL)
    everywhere = P(ALL, None)
    return jax.shard_map(
        on_device,
        mesh=split,
        in_specs=(
            P(("x", "c"), None),
            everywhere,
            everywhere,
            P(),
            P(),
            P(),
            P(("y", "z"), ("x", "c")),
        ),
        out_specs=everywhere,
        check_vma=False,
    )
```

```python
import functools

import jax
import jax.numpy as jnp
from jax import lax
from jax.experimental import pallas as pl
from jax.experimental.pallas import tpu as pltpu
from jax.sharding import Mesh
from jax.sharding import PartitionSpec as P

SEQS = 16
ALL = ("y", "z", "x", "c")
TILE = 256
LIMIT = 26 * 1024 * 1024
AHEAD = 2
BF = jnp.bfloat16
F32 = jnp.float32


def index(y, z, x, c):
    return (((y % 4) * 4 + z % 4) * 4 + x % 4) * 2 + c


def move(value, target):
    pairs = [
        (index(y, z, x, c), index(*target(y, z, x, c)))
        for y in range(4)
        for z in range(4)
        for x in range(4)
        for c in range(2)
    ]
    return lax.ppermute(value, ALL, pairs)


def along_x(y, z, x, c):
    return (y, z, x + 1 - 2 * c, c)


def along_x_crossed(y, z, x, c):
    return (y, z, x - 1 + 2 * c, 1 - c)


def along_y(y, z, x, c):
    return (y + 1 - 2 * c, z, x, c)


def along_z(y, z, x, c):
    return (y, z + 1 - 2 * c, x, c)


def to_sibling(y, z, x, c):
    return (y, z, x, 1 - c)


def rows_kernel(plan, count, *refs):
    sources, results, sems = refs[:count], refs[count:-1], refs[-1]
    copies = [
        pltpu.make_async_copy(
            sources[source].at[start : start + rows, :],
            results[to].at[at : at + rows, :],
            sems.at[n],
        )
        for n, (source, start, rows, to, at) in enumerate(plan)
    ]
    for copy in copies:
        copy.start()
    for copy in copies:
        copy.wait()


def rows_of(plan, sources, lengths, space=pl.ANY):
    away = pl.BlockSpec(memory_space=pl.ANY)
    width = sources[0].shape[1]
    return pl.pallas_call(
        functools.partial(rows_kernel, plan, len(sources)),
        in_specs=[away] * len(sources),
        out_specs=[pl.BlockSpec(memory_space=space)] * len(lengths),
        out_shape=[jax.ShapeDtypeStruct((n, width), BF) for n in lengths],
        scratch_shapes=[pltpu.SemaphoreType.DMA((len(plan),))],
        compiler_params=pltpu.CompilerParams(vmem_limit_bytes=16 * 1024 * 1024),
        cost_estimate=pl.CostEstimate(
            flops=0, bytes_accessed=4 * width * sum(lengths), transcendentals=0
        ),
    )(*sources)


def flash_kernel(sizes, stream, *refs):
    count = len(sizes)
    pieces, heads = refs[:count], refs[count : count + 2]
    projs, in_ref = refs[count + 2 : count + 4], refs[count + 4]
    out_ref, lse_ref, side_ref = refs[count + 5 : count + 8]
    tok, held, scores, sems, head_sem = refs[count + 8 : count + 13]
    rows = heads[0].shape[0]

    copies = []
    at = 0
    for number, (size, piece) in enumerate(zip(sizes, pieces)):
        copies.append(pltpu.make_async_copy(piece, tok.at[at : at + size, :], sems.at[number]))
        at += size
    blocks = []
    bounds = (0, 256, 512, 1024, 1536, 2048) if stream else (1024, 1536, 2048)
    for low, high in zip(bounds, bounds[1:]):
        head, shift = heads[low // rows], low // rows * rows
        at = low if stream else low - rows
        blocks.append(
            pltpu.make_async_copy(
                head.at[low - shift : high - shift, :],
                held.at[at : at + high - low, :],
                head_sem.at[len(blocks)],
            )
        )
    others = []
    if stream:
        far = (*projs, in_ref)
        *projs, in_ref = refs[count + 13 : count + 16]
        for n, (source, target) in enumerate(zip(far, (*projs, in_ref))):
            others.append(pltpu.make_async_copy(source, target, refs[count + 16].at[n]))
    for copy in copies + blocks[:AHEAD] + others:
        copy.start()
    for copy in copies:
        copy.wait()

    dims = (((1,), (1,)), ((), ()))
    tile = 1024 if tok.shape[0] <= 256 else 512
    if not stream:
        for low in range(0, rows, tile):
            scores[:, low : low + tile] = lax.dot_general(
                tok[...], heads[0][low : low + tile, :], dims, preferred_element_type=F32
            )
        for block in blocks:
            block.wait()
        for low in range(0, rows, tile):
            scores[:, rows + low : rows + low + tile] = lax.dot_general(
                tok[...], held[low : low + tile, :], dims, preferred_element_type=F32
            )
    else:
        for n, block in enumerate(blocks):
            block.wait()
            if n + AHEAD < len(blocks):
                blocks[n + AHEAD].start()
            low, high = bounds[n], bounds[n + 1]
            scores[:, low:high] = lax.dot_general(
                tok[...], held[low:high, :], dims, preferred_element_type=F32
            )
    for copy in others:
        copy.wait()
    side_ref[...] = jnp.dot(tok[...], in_ref[...], preferred_element_type=F32)

    step = 512
    best = scores[:, 0:step]
    for low in range(step, 2 * rows, step):
        best = jnp.maximum(best, scores[:, low : low + step])
    best = jnp.max(best, axis=1, keepdims=True)
    total = None
    mixed = None
    for low in range(0, 2 * rows, step):
        power = jnp.exp(scores[:, low : low + step] - best)
        total = power if low == 0 else total + power
        proj = projs[low // rows][low % rows : low % rows + step, :]
        part = jnp.dot(power.astype(BF), proj, preferred_element_type=F32)
        mixed = part if low == 0 else mixed + part
    total = jnp.sum(total, axis=1, keepdims=True)
    out_ref[...] = mixed / total
    lse_ref[...] = jnp.broadcast_to(best + jnp.log(total), lse_ref.shape)


def flash(pieces, own, sib, proj_own, proj_sib, in_proj, limit=None):
    sizes = tuple(p.shape[0] for p in pieces)
    n = sum(sizes)
    stream = limit is not None
    rows, depth = own.shape
    rank = proj_own.shape[1]
    here = pl.BlockSpec(memory_space=pltpu.VMEM)
    away = pl.BlockSpec(memory_space=pl.ANY)
    extra = []
    if stream:
        extra = [pltpu.VMEM(a.shape, BF) for a in (proj_own, proj_sib, in_proj)]
        extra.append(pltpu.SemaphoreType.DMA((3,)))
    return pl.pallas_call(
        functools.partial(flash_kernel, sizes, stream),
        in_specs=[away] * len(pieces) + ([away] * 5 if stream else [here, away, here, here, here]),
        out_specs=[here] * 3,
        out_shape=[jax.ShapeDtypeStruct((n, rank), F32)] * 3,
        scratch_shapes=[
            pltpu.VMEM((n, depth), BF),
            pltpu.VMEM((2 * rows if stream else rows, depth), BF),
            pltpu.VMEM((n, 2 * rows), F32),
            pltpu.SemaphoreType.DMA((len(pieces),)),
            pltpu.SemaphoreType.DMA((5 if stream else 2,)),
        ]
        + extra,
        compiler_params=pltpu.CompilerParams(vmem_limit_bytes=(limit << 20) if stream else LIMIT),
        cost_estimate=pl.CostEstimate(
            flops=2 * n * 2 * rows * depth, bytes_accessed=n * depth * 2, transcendentals=0
        ),
    )(*pieces, own, sib, proj_own, proj_sib, in_proj)


def half_kernel(with_side, tok_far, head_far, proj_far, in_far, *refs):
    count = 3 if with_side else 2
    out_ref, lse_ref = refs[:2]
    tok, held, proj, in_proj, scores, sems = refs[count:]
    rows = head_far.shape[0]
    blocks = [
        pltpu.make_async_copy(
            head_far.at[low : low + TILE, :], held.at[low : low + TILE, :], sems.at[low // TILE]
        )
        for low in range(0, rows, TILE)
    ]
    first = pltpu.make_async_copy(tok_far, tok, sems.at[4])
    others = [pltpu.make_async_copy(proj_far, proj, sems.at[5])]
    if with_side:
        others.append(pltpu.make_async_copy(in_far, in_proj, sems.at[6]))
    for copy in [first] + blocks + others:
        copy.start()
    first.wait()
    for n, block in enumerate(blocks):
        block.wait()
        low = n * TILE
        scores[:, low : low + TILE] = lax.dot_general(
            tok[...],
            held[low : low + TILE, :],
            (((1,), (1,)), ((), ())),
            preferred_element_type=F32,
        )
    for copy in others:
        copy.wait()
    if with_side:
        refs[2][...] = jnp.dot(tok[...], in_proj[...], preferred_element_type=F32)
    best = jnp.max(scores[...], axis=1, keepdims=True)
    power = jnp.exp(scores[...] - best)
    total = jnp.sum(power, axis=1, keepdims=True)
    mixed = jnp.dot(power.astype(BF), proj[...], preferred_element_type=F32)
    out_ref[...] = mixed / total
    lse_ref[...] = jnp.broadcast_to(best + jnp.log(total), lse_ref.shape)


def half(tokens, head, proj, in_proj, with_side, limit):
    n, depth = tokens.shape
    rows, rank = proj.shape
    count = 3 if with_side else 2
    return pl.pallas_call(
        functools.partial(half_kernel, with_side),
        in_specs=[pl.BlockSpec(memory_space=pl.ANY)] * 4,
        out_specs=[pl.BlockSpec(memory_space=pltpu.VMEM)] * count,
        out_shape=[jax.ShapeDtypeStruct((n, rank), F32)] * count,
        scratch_shapes=[
            pltpu.VMEM((n, depth), BF),
            pltpu.VMEM((rows, depth), BF),
            pltpu.VMEM((rows, rank), BF),
            pltpu.VMEM((depth, rank), BF),
            pltpu.VMEM((n, rows), F32),
            pltpu.SemaphoreType.DMA((7,)),
        ],
        compiler_params=pltpu.CompilerParams(vmem_limit_bytes=limit << 20),
        cost_estimate=pl.CostEstimate(
            flops=2 * n * rows * depth, bytes_accessed=rows * depth * 2, transcendentals=0
        ),
    )(tokens, head, proj, in_proj)


def hot_kernel(where, targets_ref, own_ref, sib_ref, out_ref):
    local = out_ref.shape[1]
    total = jnp.zeros(out_ref.shape, F32)
    for which, proj_ref in enumerate((own_ref, sib_ref)):
        for first in range(0, proj_ref.shape[0], TILE):
            ids = where[which] + first + lax.broadcasted_iota(jnp.int32, (TILE, local), 0)
            hot = jnp.where(ids == targets_ref[...], 1.0, 0.0).astype(BF)
            total += lax.dot_general(
                proj_ref[first : first + TILE, :],
                hot,
                (((0,), (0,)), ((), ())),
                preferred_element_type=F32,
            )
    out_ref[...] = total


def hot_rows(where, targets, proj_own, proj_sib):
    here = pl.BlockSpec(memory_space=pltpu.VMEM)
    return pl.pallas_call(
        hot_kernel,
        in_specs=[pl.BlockSpec(memory_space=pltpu.SMEM), here, here, here],
        out_specs=here,
        out_shape=jax.ShapeDtypeStruct((proj_own.shape[1], targets.shape[1]), F32),
        compiler_params=pltpu.CompilerParams(vmem_limit_bytes=16 * 1024 * 1024),
        cost_estimate=pl.CostEstimate(
            flops=2 * 128 * 2048 * 1024, bytes_accessed=1 << 20, transcendentals=0
        ),
    )(where, targets, proj_own, proj_sib)


def pack_kernel(place, *refs):
    outs, lses, sides = refs[0:3], refs[3:6], refs[6:9]
    outs, lses = list(outs), list(lses)
    more_out, more_lse, hot_ref, send_ref, side_ref, out_nat, lse_nat, out_own, lse_own = refs[9:]
    top = jnp.maximum(lses[0][...], more_lse[...])
    here = jnp.exp(lses[0][...] - top)
    there = jnp.exp(more_lse[...] - top)
    out_own[...] = (outs[0][...] * here + more_out[...] * there) / (here + there)
    lse_own[...] = top + jnp.log(here + there)
    outs[0], lses[0] = out_own, lse_own
    k = place[0]
    spot = [place[1], place[2], place[3], place[4]]

    def put(slot, quarter, source, start, rows, into=0):
        for h in range(rows // 32):
            group = quarter * 2 + into + h
            at = slice(start + 32 * h, start + 32 * h + 32)
            out_nat[group, spot[slot]] = outs[source][at, :]
            lse_nat[group, spot[slot]] = lses[source][at, :]
            side_ref[group, spot[slot]] = sides[source][at, :]

    ky, kz, kd = k ^ 2, k ^ 1, k ^ 3
    for q in range(4):
        put(0, q, 0, 64 * q, 64)
    for n, (slot, quarter) in enumerate(
        [(1, k), (2, k), (1, ky), (2, ky), (1, kz), (2, kz), (3, k), (1, kd)]
    ):
        put(slot, quarter, 1, 64 * n, 64)
    put(3, ky, 2, 0, 64)
    put(2, kd, 2, 64, 32)
    put(3, kz, 2, 96, 64)
    put(2, kd, 2, 160, 32, into=1)
    put(3, kd, 2, 192, 64)

    for group in range(8):
        mixed = jnp.transpose(out_nat[group].reshape(128, 128)).reshape(16, 8, 128)
        lse = jnp.transpose(lse_nat[group].reshape(128, 128))[0:8, :]
        high = lse.astype(BF).astype(F32)
        rest = lse - high
        middle = rest.astype(BF).astype(F32)
        low = rest - middle
        line = lax.broadcasted_iota(jnp.int32, (8, 128), 0)
        stats = jnp.where(
            line == 0, high, jnp.where(line == 1, middle, jnp.where(line == 2, low, 0.0))
        )
        hot = hot_ref[:, group * 128 : group * 128 + 128].reshape(16, 8, 128)
        for part in range(16):
            to = (2 * group + part % 2) * 8 + part // 2
            send_ref[to] = jnp.concatenate([mixed[part], hot[part], stats], axis=0).astype(BF)


def pack(place, results, more, hot):
    outs, lses, sides = zip(*results)
    return pl.pallas_call(
        pack_kernel,
        in_specs=[pl.BlockSpec(memory_space=pltpu.SMEM)]
        + [pl.BlockSpec(memory_space=pltpu.VMEM)] * 12,
        out_specs=[pl.BlockSpec(memory_space=pltpu.VMEM)] * 2,
        out_shape=[
            jax.ShapeDtypeStruct((128, 24, 128), BF),
            jax.ShapeDtypeStruct((8, 4, 32, 128), F32),
        ],
        scratch_shapes=[pltpu.VMEM((8, 4, 32, 128), F32)] * 2 + [pltpu.VMEM((256, 128), F32)] * 2,
        compiler_params=pltpu.CompilerParams(vmem_limit_bytes=16 * 1024 * 1024),
    )(place, *outs, *lses, *sides, *more, hot)


def merge_kernel(got_ref, out_ref):
    lse = (
        got_ref[:, 16:24, :].astype(F32)
    )
    lse = lse[:, 0:1, :] + lse[:, 1:2, :] + lse[:, 2:3, :]
    source = lax.broadcasted_iota(jnp.int32, (128, 1, 128), 0)
    lane = lax.broadcasted_iota(jnp.int32, (128, 1, 128), 2)
    x = lax.div(lax.rem(source, 8), 2)
    c = lax.rem(source, 2)
    other = lax.div(lane, 32) == lax.rem(x + 1, 4)
    kind = jnp.where(other, 1 - c, c)
    halves = []
    for which in range(2):
        mine = kind == which
        best = jnp.max(jnp.where(mine, lse, -3.0e38), axis=0, keepdims=True)
        weight = jnp.where(mine, jnp.exp(jnp.minimum(lse - best, 0.0)), 0.0)
        total = jnp.sum(weight, axis=0)
        mixed = jnp.sum(weight * got_ref[:, 0:8, :].astype(F32), axis=0)
        hot = jnp.sum(jnp.where(mine, got_ref[:, 8:16, :].astype(F32), 0.0), axis=0)
        halves.append(mixed / total - hot)
    both = jnp.concatenate(halves, axis=1)
    for copy in range(16):
        out_ref[copy] = both


def merge(got):
    return pl.pallas_call(
        merge_kernel,
        in_specs=[pl.BlockSpec(memory_space=pltpu.VMEM)],
        out_specs=pl.BlockSpec(memory_space=pltpu.VMEM),
        out_shape=jax.ShapeDtypeStruct((16, 8, 256), F32),
        compiler_params=pltpu.CompilerParams(vmem_limit_bytes=16 * 1024 * 1024),
    )(got)


def score_kernel(
    flags, out_ref, own_hbm, sib_hbm, seq_ref, store_ref, result_ref, own_ref, sib_ref, store, sems, side_sem
):
    rows = store.shape[0] // 8
    copies = [
        pltpu.make_async_copy(
            store_ref.at[n * rows : (n + 1) * rows, :],
            store.at[n * rows : (n + 1) * rows, :],
            sems.at[n],
        )
        for n in range(8)
    ]
    sides = [
        pltpu.make_async_copy(own_hbm, own_ref, side_sem.at[0]),
        pltpu.make_async_copy(sib_hbm, sib_ref, side_sem.at[1]),
    ]
    for copy in sides + copies[:3]:
        copy.start()
    for copy in sides:
        copy.wait()
    total = jnp.zeros((256, 128), F32)
    for group in range(8):
        out = jnp.concatenate([out_ref[2 * group], out_ref[2 * group + 1]], axis=0)
        ids = seq_ref[group : group + 1, :]
        member = lax.broadcasted_iota(jnp.int32, (16, 256), 0) == ids
        spread = jnp.where(member[None, :, :], out[:, None, :], 0.0).reshape(256, 256)
        first, second = [], []
        for spot in range(4):
            own, sib = own_ref[group, spot], sib_ref[group, spot]
            keep = flags[spot] == 0
            first.append(jnp.where(keep, own, sib))
            second.append(jnp.where(keep, sib, own))
        side = jnp.concatenate(first + second, axis=0)
        spread_high = spread.astype(BF)
        spread_low = (spread - spread_high.astype(F32)).astype(BF)
        side_high = side.astype(BF)
        side_low = (side - side_high.astype(F32)).astype(BF)
        for a, b in (
            (spread_high, side_high),
            (spread_high, side_low),
            (spread_low, side_high),
        ):
            total += jnp.dot(a, b, preferred_element_type=F32)
    grads = jnp.concatenate(
        [total[i * 16 : (i + 1) * 16, :].astype(BF) for i in range(16)], axis=1
    )
    for n, copy in enumerate(copies):
        copy.wait()
        if n + 3 < 8:
            copies[n + 3].start()
        result_ref[n] = lax.dot_general(
            grads,
            store[n * rows : (n + 1) * rows, :],
            (((1,), (1,)), ((), ())),
            preferred_element_type=F32,
        )


def score(flags, out, own, sib, seq, store):
    here = pl.BlockSpec(memory_space=pltpu.VMEM)
    away = pl.BlockSpec(memory_space=pl.ANY)
    return pl.pallas_call(
        score_kernel,
        in_specs=[
            pl.BlockSpec(memory_space=pltpu.SMEM),
            here,
            away,
            away,
            here,
            away,
        ],
        out_specs=here,
        out_shape=jax.ShapeDtypeStruct((8, SEQS, store.shape[0] // 8), F32),
        scratch_shapes=[
            pltpu.VMEM(own.shape, F32),
            pltpu.VMEM(own.shape, F32),
            pltpu.VMEM(store.shape, BF),
            pltpu.SemaphoreType.DMA((8,)),
            pltpu.SemaphoreType.DMA((2,)),
        ],
        compiler_params=pltpu.CompilerParams(vmem_limit_bytes=48 * 1024 * 1024),
    )(flags, out, own, sib, seq, store)


def by_place(per_token):
    table = per_token.reshape(4, 2, 256)
    return jnp.stack([table[:, 0], jnp.roll(table[:, 1], 2, axis=0)])


def on_device(hidden, out_head, out_proj, in_proj, targets, seq_ids, grad_store):
    y, z, x, c = (lax.axis_index(name) for name in ALL)
    k = 2 * (y % 2) + z % 2
    sign = 1 - 2 * c
    rows = out_head.shape[0]

    mine = lax.dynamic_slice_in_dim(hidden, k * 64, 64, 0)

    near_a = move(mine, along_x)
    near_b = move(mine, along_x_crossed)
    head_sib = move(out_head, to_sibling)
    proj_sib = move(out_proj, to_sibling)

    first_row = lax.axis_index(ALL) * rows
    sib_row = (lax.axis_index(ALL) + sign) * rows
    places = jnp.arange(4, dtype=jnp.int32)
    kinds = jnp.where(places == (x + 1) % 4, 1 - c, c)
    target_table = by_place(targets)
    local_targets = jnp.where(kinds[:, None] == 0, target_table[0], target_table[1])
    local_targets = local_targets.reshape(4, 8, 32).transpose(1, 0, 2).reshape(1, 1024)
    seq_table = by_place(seq_ids).reshape(2, 4, 8, 32).transpose(2, 0, 1, 3).reshape(8, 256)

    again, local_targets = lax.optimization_barrier((hidden, local_targets))
    mine_d = lax.dynamic_slice_in_dim(again, (3 - k) * 64, 64, 0)

    first = half(hidden, out_head, out_proj, in_proj, True, 50)
    mine_d, near_a, proj_sib, first = lax.optimization_barrier((mine_d, near_a, proj_sib, first))
    near, ahead = rows_of(
        ((0, 0, 64, 0, 0), (1, 0, 64, 0, 64), (0, 0, 64, 1, 0), (2, 0, 64, 1, 64)),
        [near_a, near_b, mine_d],
        [128, 128],
        pltpu.VMEM,
    )
    near_y = move(near, along_y)
    near_z = move(near, along_z)
    ahead = move(ahead, along_x)
    rest = (out_head, head_sib, out_proj, proj_sib, in_proj)
    more = half(hidden, head_sib, proj_sib, in_proj, False, 24)
    more, ahead, near_y, near_z = lax.optimization_barrier((more, ahead, near_y, near_z))
    more, local_targets = lax.optimization_barrier((more, local_targets))
    hot = hot_rows(jnp.stack([first_row, sib_row]), local_targets, out_proj, proj_sib)
    last_y, last_z, far_d = rows_of(
        (
            (0, 0, 64, 0, 0),
            (2, 64, 32, 0, 64),
            (0, 0, 64, 1, 0),
            (1, 96, 32, 1, 64),
            (0, 64, 64, 2, 0),
        ),
        [ahead, near_y, near_z],
        [96, 96, 64],
    )
    last_y = move(last_y, along_y)
    last_z = move(last_z, along_z)
    far_d = move(far_d, along_x)
    second = flash([near, near_y, near_z, ahead], *rest)
    third = flash([last_y, last_z, far_d], *rest)
    place = jnp.stack(
        [
            k,
            (x + 2 * c) % 4,
            (x - sign + 2 * c + 4) % 4,
            (x - sign + 2 * (1 - c) + 4) % 4,
            (x + 2 + 2 * c) % 4,
        ]
    ).astype(jnp.int32)
    send, side = pack(place, (first, second, third), more, hot)
    side_sib = move(side, to_sibling)

    got = lax.all_to_all(send, ALL, 0, 0, tiled=True)

    out = lax.all_to_all(merge(got), ("y", "z"), 0, 0, tiled=True)
    partial = score(kinds.astype(jnp.int32), out, side, side_sib, seq_table, grad_store)
    return jnp.sum(lax.all_to_all(partial, ("x", "c"), 0, 0, tiled=True), axis=0).T


def solution(mesh):
    split = Mesh(mesh.devices.reshape(4, 4, 4, 2), ALL)
    everywhere = P(ALL, None)
    return jax.shard_map(
        on_device,
        mesh=split,
        in_specs=(
            P(("x", "c"), None),
            everywhere,
            everywhere,
            P(),
            P(),
            P(),
            P(("y", "z"), ("x", "c")),
        ),
        out_specs=everywhere,
        check_vma=False,
    )
```

```python
import functools

import jax
import jax.numpy as jnp
from jax import lax
from jax.experimental import pallas as pl
from jax.experimental.pallas import tpu as pltpu
from jax.sharding import Mesh
from jax.sharding import PartitionSpec as P

SEQS = 16
ALL = ("y", "z", "x", "c")
TILE = 256
LIMIT = 26 * 1024 * 1024
AHEAD = 2
BF = jnp.bfloat16
F32 = jnp.float32


def index(y, z, x, c):
    return (((y % 4) * 4 + z % 4) * 4 + x % 4) * 2 + c


def move(value, target):
    pairs = [
        (index(y, z, x, c), index(*target(y, z, x, c)))
        for y in range(4)
        for z in range(4)
        for x in range(4)
        for c in range(2)
    ]
    return lax.ppermute(value, ALL, pairs)


def along_x(y, z, x, c):
    return (y, z, x + 1 - 2 * c, c)


def along_x_crossed(y, z, x, c):
    return (y, z, x - 1 + 2 * c, 1 - c)


def along_y(y, z, x, c):
    return (y + 1 - 2 * c, z, x, c)


def along_z(y, z, x, c):
    return (y, z + 1 - 2 * c, x, c)


def to_sibling(y, z, x, c):
    return (y, z, x, 1 - c)


def rows_kernel(plan, count, *refs):
    sources, results, sems = refs[:count], refs[count:-1], refs[-1]
    copies = [
        pltpu.make_async_copy(
            sources[source].at[start : start + rows, :],
            results[to].at[at : at + rows, :],
            sems.at[n],
        )
        for n, (source, start, rows, to, at) in enumerate(plan)
    ]
    for copy in copies:
        copy.start()
    for copy in copies:
        copy.wait()


def rows_of(plan, sources, lengths):
    away = pl.BlockSpec(memory_space=pl.ANY)
    width = sources[0].shape[1]
    return pl.pallas_call(
        functools.partial(rows_kernel, plan, len(sources)),
        in_specs=[away] * len(sources),
        out_specs=[away] * len(lengths),
        out_shape=[jax.ShapeDtypeStruct((n, width), BF) for n in lengths],
        scratch_shapes=[pltpu.SemaphoreType.DMA((len(plan),))],
        compiler_params=pltpu.CompilerParams(vmem_limit_bytes=16 * 1024 * 1024),
        cost_estimate=pl.CostEstimate(
            flops=0, bytes_accessed=4 * width * sum(lengths), transcendentals=0
        ),
    )(*sources)


def flash_kernel(sizes, stream, *refs):
    count = len(sizes)
    pieces, heads = refs[:count], refs[count : count + 2]
    projs, in_ref = refs[count + 2 : count + 4], refs[count + 4]
    out_ref, lse_ref, side_ref = refs[count + 5 : count + 8]
    tok, held, scores, sems, head_sem = refs[count + 8 : count + 13]
    rows = heads[0].shape[0]

    copies = []
    at = 0
    for number, (size, piece) in enumerate(zip(sizes, pieces)):
        copies.append(pltpu.make_async_copy(piece, tok.at[at : at + size, :], sems.at[number]))
        at += size
    blocks = []
    bounds = (0, 256, 512, 1024, 1536, 2048) if stream else (1024, 1536, 2048)
    for low, high in zip(bounds, bounds[1:]):
        head, shift = heads[low // rows], low // rows * rows
        at = low if stream else low - rows
        blocks.append(
            pltpu.make_async_copy(
                head.at[low - shift : high - shift, :],
                held.at[at : at + high - low, :],
                head_sem.at[len(blocks)],
            )
        )
    others = []
    if stream:
        far = (*projs, in_ref)
        *projs, in_ref = refs[count + 13 : count + 16]
        for n, (source, target) in enumerate(zip(far, (*projs, in_ref))):
            others.append(pltpu.make_async_copy(source, target, refs[count + 16].at[n]))
    for copy in copies + blocks[:AHEAD] + others:
        copy.start()
    for copy in copies:
        copy.wait()

    dims = (((1,), (1,)), ((), ()))
    tile = 1024 if tok.shape[0] <= 256 else 512
    step = 512

    def softmax_part(which):
        first, last = which * rows, (which + 1) * rows
        best = scores[:, first : first + step]
        for low in range(first + step, last, step):
            best = jnp.maximum(best, scores[:, low : low + step])
        best = jnp.max(best, axis=1, keepdims=True)
        total = None
        mixed = None
        for low in range(first, last, step):
            power = jnp.exp(scores[:, low : low + step] - best)
            total = power if low == first else total + power
            proj = projs[which][low - first : low - first + step, :]
            part = jnp.dot(power.astype(BF), proj, preferred_element_type=F32)
            mixed = part if low == first else mixed + part
        return best, jnp.sum(total, axis=1, keepdims=True), mixed

    for low in range(0, rows, tile):
        scores[:, low : low + tile] = lax.dot_general(
            tok[...], heads[0][low : low + tile, :], dims, preferred_element_type=F32
        )
    for block in blocks:
        block.wait()
    best_a, total_a, mixed_a = softmax_part(0)
    for low in range(0, rows, tile):
        scores[:, rows + low : rows + low + tile] = lax.dot_general(
            tok[...], held[low : low + tile, :], dims, preferred_element_type=F32
        )
    side_ref[...] = jnp.dot(tok[...], in_ref[...], preferred_element_type=F32)
    best_b, total_b, mixed_b = softmax_part(1)
    best = jnp.maximum(best_a, best_b)
    scale_a = jnp.exp(best_a - best)
    scale_b = jnp.exp(best_b - best)
    total = total_a * scale_a + total_b * scale_b
    out_ref[...] = (mixed_a * scale_a + mixed_b * scale_b) / total
    lse_ref[...] = jnp.broadcast_to(best + jnp.log(total), lse_ref.shape)


def flash(pieces, own, sib, proj_own, proj_sib, in_proj, limit=None):
    sizes = tuple(p.shape[0] for p in pieces)
    n = sum(sizes)
    stream = limit is not None
    rows, depth = own.shape
    rank = proj_own.shape[1]
    here = pl.BlockSpec(memory_space=pltpu.VMEM)
    away = pl.BlockSpec(memory_space=pl.ANY)
    extra = []
    if stream:
        extra = [pltpu.VMEM(a.shape, BF) for a in (proj_own, proj_sib, in_proj)]
        extra.append(pltpu.SemaphoreType.DMA((3,)))
    return pl.pallas_call(
        functools.partial(flash_kernel, sizes, stream),
        in_specs=[away] * len(pieces) + ([away] * 5 if stream else [here, away, here, here, here]),
        out_specs=[here] * 3,
        out_shape=[jax.ShapeDtypeStruct((n, rank), F32)] * 3,
        scratch_shapes=[
            pltpu.VMEM((n, depth), BF),
            pltpu.VMEM((2 * rows if stream else rows, depth), BF),
            pltpu.VMEM((n, 2 * rows), F32),
            pltpu.SemaphoreType.DMA((len(pieces),)),
            pltpu.SemaphoreType.DMA((5 if stream else 2,)),
        ]
        + extra,
        compiler_params=pltpu.CompilerParams(vmem_limit_bytes=(limit << 20) if stream else LIMIT),
        cost_estimate=pl.CostEstimate(
            flops=2 * n * 2 * rows * depth, bytes_accessed=n * depth * 2, transcendentals=0
        ),
    )(*pieces, own, sib, proj_own, proj_sib, in_proj)


def hot_kernel(where, targets_ref, own_ref, sib_ref, out_ref):
    local = out_ref.shape[1]
    total = jnp.zeros(out_ref.shape, F32)
    for which, proj_ref in enumerate((own_ref, sib_ref)):
        for first in range(0, proj_ref.shape[0], TILE):
            ids = where[which] + first + lax.broadcasted_iota(jnp.int32, (TILE, local), 0)
            hot = jnp.where(ids == targets_ref[...], 1.0, 0.0).astype(BF)
            total += lax.dot_general(
                proj_ref[first : first + TILE, :],
                hot,
                (((0,), (0,)), ((), ())),
                preferred_element_type=F32,
            )
    out_ref[...] = total


def hot_rows(where, targets, proj_own, proj_sib):
    here = pl.BlockSpec(memory_space=pltpu.VMEM)
    return pl.pallas_call(
        hot_kernel,
        in_specs=[pl.BlockSpec(memory_space=pltpu.SMEM), here, here, here],
        out_specs=here,
        out_shape=jax.ShapeDtypeStruct((proj_own.shape[1], targets.shape[1]), F32),
        compiler_params=pltpu.CompilerParams(vmem_limit_bytes=16 * 1024 * 1024),
        cost_estimate=pl.CostEstimate(
            flops=2 * 128 * 2048 * 1024, bytes_accessed=1 << 20, transcendentals=0
        ),
    )(where, targets, proj_own, proj_sib)


def pack_kernel(place, *refs):
    outs, lses, sides = refs[0:3], refs[3:6], refs[6:9]
    hot_ref, send_ref, side_ref, out_nat, lse_nat = refs[9:]
    k = place[0]
    spot = [place[1], place[2], place[3], place[4]]

    def put(slot, quarter, source, start, rows, into=0):
        for h in range(rows // 32):
            group = quarter * 2 + into + h
            at = slice(start + 32 * h, start + 32 * h + 32)
            out_nat[group, spot[slot]] = outs[source][at, :]
            lse_nat[group, spot[slot]] = lses[source][at, :]
            side_ref[group, spot[slot]] = sides[source][at, :]

    ky, kz, kd = k ^ 2, k ^ 1, k ^ 3
    for q in range(4):
        put(0, q, 0, 64 * q, 64)
    for n, (slot, quarter) in enumerate(
        [(1, k), (2, k), (1, ky), (2, ky), (1, kz), (2, kz), (3, k), (1, kd)]
    ):
        put(slot, quarter, 1, 64 * n, 64)
    put(3, ky, 2, 0, 64)
    put(2, kd, 2, 64, 32)
    put(3, kz, 2, 96, 64)
    put(2, kd, 2, 160, 32, into=1)
    put(3, kd, 2, 192, 64)

    for group in range(8):
        mixed = jnp.transpose(out_nat[group].reshape(128, 128)).reshape(16, 8, 128)
        lse = jnp.transpose(lse_nat[group].reshape(128, 128))[0:8, :]
        high = lse.astype(BF).astype(F32)
        rest = lse - high
        middle = rest.astype(BF).astype(F32)
        low = rest - middle
        line = lax.broadcasted_iota(jnp.int32, (8, 128), 0)
        stats = jnp.where(
            line == 0, high, jnp.where(line == 1, middle, jnp.where(line == 2, low, 0.0))
        )
        hot = hot_ref[:, group * 128 : group * 128 + 128].reshape(16, 8, 128)
        for part in range(16):
            to = (2 * group + part % 2) * 8 + part // 2
            send_ref[to] = jnp.concatenate([mixed[part], hot[part], stats], axis=0).astype(BF)


def pack(place, results, hot):
    outs, lses, sides = zip(*results)
    return pl.pallas_call(
        pack_kernel,
        in_specs=[pl.BlockSpec(memory_space=pltpu.SMEM)]
        + [pl.BlockSpec(memory_space=pltpu.VMEM)] * 10,
        out_specs=[pl.BlockSpec(memory_space=pltpu.VMEM)] * 2,
        out_shape=[
            jax.ShapeDtypeStruct((128, 24, 128), BF),
            jax.ShapeDtypeStruct((8, 4, 32, 128), F32),
        ],
        scratch_shapes=[pltpu.VMEM((8, 4, 32, 128), F32)] * 2,
        compiler_params=pltpu.CompilerParams(vmem_limit_bytes=16 * 1024 * 1024),
    )(place, *outs, *lses, *sides, hot)


def merge_kernel(got_ref, out_ref):
    lse = (
        got_ref[:, 16:24, :].astype(F32)
    )
    lse = lse[:, 0:1, :] + lse[:, 1:2, :] + lse[:, 2:3, :]
    source = lax.broadcasted_iota(jnp.int32, (128, 1, 128), 0)
    lane = lax.broadcasted_iota(jnp.int32, (128, 1, 128), 2)
    x = lax.div(lax.rem(source, 8), 2)
    c = lax.rem(source, 2)
    other = lax.div(lane, 32) == lax.rem(x + 1, 4)
    kind = jnp.where(other, 1 - c, c)
    halves = []
    for which in range(2):
        mine = kind == which
        best = jnp.max(jnp.where(mine, lse, -3.0e38), axis=0, keepdims=True)
        weight = jnp.where(mine, jnp.exp(jnp.minimum(lse - best, 0.0)), 0.0)
        total = jnp.sum(weight, axis=0)
        mixed = jnp.sum(weight * got_ref[:, 0:8, :].astype(F32), axis=0)
        hot = jnp.sum(jnp.where(mine, got_ref[:, 8:16, :].astype(F32), 0.0), axis=0)
        halves.append(mixed / total - hot)
    both = jnp.concatenate(halves, axis=1)
    for copy in range(16):
        out_ref[copy] = both


def merge(got):
    return pl.pallas_call(
        merge_kernel,
        in_specs=[pl.BlockSpec(memory_space=pltpu.VMEM)],
        out_specs=pl.BlockSpec(memory_space=pltpu.VMEM),
        out_shape=jax.ShapeDtypeStruct((16, 8, 256), F32),
        compiler_params=pltpu.CompilerParams(vmem_limit_bytes=16 * 1024 * 1024),
    )(got)


def score_kernel(
    flags, out_ref, own_hbm, sib_hbm, seq_ref, store_ref, result_ref, own_ref, sib_ref, store, sems, side_sem
):
    rows = store.shape[0] // 8
    copies = [
        pltpu.make_async_copy(
            store_ref.at[n * rows : (n + 1) * rows, :],
            store.at[n * rows : (n + 1) * rows, :],
            sems.at[n],
        )
        for n in range(8)
    ]
    sides = [
        pltpu.make_async_copy(own_hbm, own_ref, side_sem.at[0]),
        pltpu.make_async_copy(sib_hbm, sib_ref, side_sem.at[1]),
    ]
    for copy in sides + copies[:3]:
        copy.start()
    for copy in sides:
        copy.wait()
    total = jnp.zeros((256, 128), F32)
    for group in range(8):
        out = jnp.concatenate([out_ref[2 * group], out_ref[2 * group + 1]], axis=0)
        ids = seq_ref[group : group + 1, :]
        member = lax.broadcasted_iota(jnp.int32, (16, 256), 0) == ids
        spread = jnp.where(member[None, :, :], out[:, None, :], 0.0).reshape(256, 256)
        first, second = [], []
        for spot in range(4):
            own, sib = own_ref[group, spot], sib_ref[group, spot]
            keep = flags[spot] == 0
            first.append(jnp.where(keep, own, sib))
            second.append(jnp.where(keep, sib, own))
        side = jnp.concatenate(first + second, axis=0)
        spread_high = spread.astype(BF)
        spread_low = (spread - spread_high.astype(F32)).astype(BF)
        side_high = side.astype(BF)
        side_low = (side - side_high.astype(F32)).astype(BF)
        for a, b in (
            (spread_high, side_high),
            (spread_high, side_low),
            (spread_low, side_high),
        ):
            total += jnp.dot(a, b, preferred_element_type=F32)
    grads = jnp.concatenate(
        [total[i * 16 : (i + 1) * 16, :].astype(BF) for i in range(16)], axis=1
    )
    for n, copy in enumerate(copies):
        copy.wait()
        if n + 3 < 8:
            copies[n + 3].start()
        result_ref[n] = lax.dot_general(
            grads,
            store[n * rows : (n + 1) * rows, :],
            (((1,), (1,)), ((), ())),
            preferred_element_type=F32,
        )


def score(flags, out, own, sib, seq, store):
    here = pl.BlockSpec(memory_space=pltpu.VMEM)
    away = pl.BlockSpec(memory_space=pl.ANY)
    return pl.pallas_call(
        score_kernel,
        in_specs=[
            pl.BlockSpec(memory_space=pltpu.SMEM),
            here,
            away,
            away,
            here,
            away,
        ],
        out_specs=here,
        out_shape=jax.ShapeDtypeStruct((8, SEQS, store.shape[0] // 8), F32),
        scratch_shapes=[
            pltpu.VMEM(own.shape, F32),
            pltpu.VMEM(own.shape, F32),
            pltpu.VMEM(store.shape, BF),
            pltpu.SemaphoreType.DMA((8,)),
            pltpu.SemaphoreType.DMA((2,)),
        ],
        compiler_params=pltpu.CompilerParams(vmem_limit_bytes=48 * 1024 * 1024),
    )(flags, out, own, sib, seq, store)


def by_place(per_token):
    table = per_token.reshape(4, 2, 256)
    return jnp.stack([table[:, 0], jnp.roll(table[:, 1], 2, axis=0)])


def on_device(hidden, out_head, out_proj, in_proj, targets, seq_ids, grad_store):
    y, z, x, c = (lax.axis_index(name) for name in ALL)
    k = 2 * (y % 2) + z % 2
    sign = 1 - 2 * c
    rows = out_head.shape[0]

    mine = lax.dynamic_slice_in_dim(hidden, k * 64, 64, 0)

    near_a = move(mine, along_x)
    near_b = move(mine, along_x_crossed)
    head_sib = move(out_head, to_sibling)
    proj_sib = move(out_proj, to_sibling)

    first_row = lax.axis_index(ALL) * rows
    sib_row = (lax.axis_index(ALL) + sign) * rows
    places = jnp.arange(4, dtype=jnp.int32)
    kinds = jnp.where(places == (x + 1) % 4, 1 - c, c)
    target_table = by_place(targets)
    local_targets = jnp.where(kinds[:, None] == 0, target_table[0], target_table[1])
    local_targets = local_targets.reshape(4, 8, 32).transpose(1, 0, 2).reshape(1, 1024)
    seq_table = by_place(seq_ids).reshape(2, 4, 8, 32).transpose(2, 0, 1, 3).reshape(8, 256)

    again, local_targets = lax.optimization_barrier((hidden, local_targets))
    mine_d = lax.dynamic_slice_in_dim(again, (3 - k) * 64, 64, 0)

    mine_d, near_a, proj_sib = lax.optimization_barrier((mine_d, near_a, proj_sib))
    near, ahead = rows_of(
        ((0, 0, 64, 0, 0), (1, 0, 64, 0, 64), (0, 0, 64, 1, 0), (2, 0, 64, 1, 64)),
        [near_a, near_b, mine_d],
        [128, 128],
    )
    near_y = move(near, along_y)
    near_z = move(near, along_z)
    ahead = move(ahead, along_x)
    rest = (out_head, head_sib, out_proj, proj_sib, in_proj)
    first = flash([hidden], *rest)
    first, ahead, near_y, near_z = lax.optimization_barrier((first, ahead, near_y, near_z))
    first, local_targets = lax.optimization_barrier((first, local_targets))
    hot = hot_rows(jnp.stack([first_row, sib_row]), local_targets, out_proj, proj_sib)
    last_y, last_z, far_d = rows_of(
        (
            (0, 0, 64, 0, 0),
            (2, 64, 32, 0, 64),
            (0, 0, 64, 1, 0),
            (1, 96, 32, 1, 64),
            (0, 64, 64, 2, 0),
        ),
        [ahead, near_y, near_z],
        [96, 96, 64],
    )
    last_y = move(last_y, along_y)
    last_z = move(last_z, along_z)
    far_d = move(far_d, along_x)
    second = flash([near, near_y, near_z, ahead], *rest)
    third = flash([last_y, last_z, far_d], *rest)
    place = jnp.stack(
        [
            k,
            (x + 2 * c) % 4,
            (x - sign + 2 * c + 4) % 4,
            (x - sign + 2 * (1 - c) + 4) % 4,
            (x + 2 + 2 * c) % 4,
        ]
    ).astype(jnp.int32)
    send, side = pack(place, (first, second, third), hot)
    side_sib = move(side, to_sibling)

    got = lax.all_to_all(send, ALL, 0, 0, tiled=True)

    out = lax.all_to_all(merge(got), ("y", "z"), 0, 0, tiled=True)
    partial = score(kinds.astype(jnp.int32), out, side, side_sib, seq_table, grad_store)
    return jnp.sum(lax.all_to_all(partial, ("x", "c"), 0, 0, tiled=True), axis=0).T


def solution(mesh):
    split = Mesh(mesh.devices.reshape(4, 4, 4, 2), ALL)
    everywhere = P(ALL, None)
    return jax.shard_map(
        on_device,
        mesh=split,
        in_specs=(
            P(("x", "c"), None),
            everywhere,
            everywhere,
            P(),
            P(),
            P(),
            P(("y", "z"), ("x", "c")),
        ),
        out_specs=everywhere,
        check_vma=False,
    )
```
